128 devices in a mesh: space: 16 (over y, x_hi, core), vec: 8 (over x_lo, z).
Axes of the slice: x: 4 (x_hi: 2, x_lo: 2; x = x_hi * 2 + x_lo), y: 4, z: 4, core: 2. Of those that a mesh axis runs over, the one named last changes fastest.
Arguments:
- vectors: float32 [2, 3, 384, 16, 2048], P(None, None, 'vec', 'space'), may hold values from -0.375 to 0.375
- links: float32 [3, 2, 3, 3, 16, 2048], P(None, None, None, None, 'space'), may hold values from -3.5 to 3.5
- momenta: int32 [2, 3], replicated, may hold values from -2 to 2
- directions: int32 [3], replicated, may hold values from 0 to 2, each once
Outputs:
- elementals: float32 [2, 3, 2, 384, 384], P(None, None, None, 'space', 'vec')
The draws below stay inside these ranges and needn't reach their ends.
Inputs may be any that keep to these rules, and one draw needn't show every extreme that they name: directions holds each of 0, 1, 2 once.
All inputs are finite; a program needn't handle non-finite values.
Results may differ from the reference program's by a relative error of at most 0.000098.
Values sent between devices are 32-bit elements; how exact they have to be, the bound alone decides.
A program may use at most 128 MiB of HBM per device.

```python
import jax
import jax.numpy as jnp
from jax import lax

NV = 384
LY = 32
LZ = 64
NMOM = 2
LX = 16


def plant(entries, own_key, low, high):
    longest = entries.shape.index(max(entries.shape))
    spots = []
    for shift in (0, 1):
        where = [jax.random.randint(jax.random.fold_in(own_key, axis), (), 0, length) for axis, length in enumerate(entries.shape)]
        where[longest] = (where[longest] + shift) % entries.shape[longest]
        spots.append(tuple(where))
    return entries.at[spots[0]].set(low).at[spots[1]].set(high)


def block_levels(own_key, dims, pieces, low, largest):
    level = 1.0
    for dim, parts in pieces:
        draws = jax.random.uniform(jax.random.fold_in(jax.random.fold_in(own_key, 6), dim), (parts,), jnp.float32, low / len(pieces), largest / len(pieces))
        level = level * jnp.repeat(jnp.exp(draws), dims[dim] // parts).reshape((-1,) + (1,) * (len(dims) - 1 - dim))
    return level


def bell_draw(rng, extent, deviation, most, shards=(), kind=jnp.bfloat16):
    values = deviation * jax.random.normal(rng, extent, jnp.float32)
    if shards:
        values = values * block_levels(rng, extent, shards, -0.22, 0.18)
    return jnp.clip(values, -most, most).astype(kind)


def setup_inputs(seed: int = 0) -> dict:
    seeds = jax.random.split(jax.random.key(seed), 5)
    vectors = bell_draw(seeds[0], (2, 3, NV, LX, LY * LZ), 0.06, 0.375, ((2, 8), (3, 16)), jnp.float32)
    links = bell_draw(seeds[1], (3, 2, 3, 3, LX, LY * LZ), 0.577, 3.5, ((4, 16),), jnp.float32)
    momenta = plant(jax.random.randint(seeds[2], (NMOM, 3), -2, 3), jax.random.fold_in(seeds[2], 1), -2, 2).astype(jnp.int32)
    directions = jax.random.permutation(seeds[3], 3).astype(jnp.int32)
    return dict(vectors=vectors, links=links, momenta=momenta, directions=directions)


def site_shift(field, mu, step):
    if mu == 0:
        return jnp.roll(field, -step, axis=-2)
    shape = field.shape
    cube = field.reshape(shape[:-1] + (LY, LZ))
    cube = jnp.roll(cube, -step, axis=-3 + mu)
    return cube.reshape(shape)


def color_apply(link, field, dagger):
    link_re = link[0]
    link_im = link[1]
    if dagger:
        link_re = jnp.swapaxes(link_re, 0, 1)
        link_im = -jnp.swapaxes(link_im, 0, 1)
    link_re = link_re[:, :, None]
    link_im = link_im[:, :, None]
    field_re = field[0][None]
    field_im = field[1][None]
    out_re = jnp.sum(link_re * field_re - link_im * field_im, axis=1)
    out_im = jnp.sum(link_re * field_im + link_im * field_re, axis=1)
    return jnp.stack([out_re, out_im], 0)


def displace(vectors, links, mu):
    forward = color_apply(links[mu], site_shift(vectors, mu, 1), False)
    backward = site_shift(color_apply(links[mu], vectors, True), mu, -1)
    return forward - backward


def phase_tables(momenta, xcoord, sites):
    ycoord = sites // LZ
    zcoord = sites % LZ
    p0 = momenta[:, 0][:, None, None]
    p1 = momenta[:, 1][:, None, None]
    p2 = momenta[:, 2][:, None, None]
    frac = ((p0 * xcoord[None]) % LX).astype(jnp.float32) / LX
    frac = frac + ((p1 * ycoord[None, None]) % LY).astype(jnp.float32) / LY
    frac = frac + ((p2 * zcoord[None, None]) % LZ).astype(jnp.float32) / LZ
    theta = 2.0 * jnp.pi * frac
    return jnp.cos(theta), jnp.sin(theta)


def elemental_block(left_vecs, right_disp, cosine, sine):
    vec_re = left_vecs[0][None]
    vec_im = left_vecs[1][None]
    cosine = cosine[:, None, None]
    sine = sine[:, None, None]
    left_re = vec_re * cosine - vec_im * sine
    left_im = -(vec_re * sine + vec_im * cosine)
    left = jnp.stack([left_re, left_im], 1)
    gram = jnp.einsum("mpcaxs,dqcbxs->mpadqb", left, right_disp, precision=lax.Precision.HIGHEST, preferred_element_type=jnp.float32)
    part_re = gram[:, 0, :, :, 0] - gram[:, 1, :, :, 1]
    part_im = gram[:, 0, :, :, 1] + gram[:, 1, :, :, 0]
    stacked = jnp.stack([part_re, part_im], 1)
    return jnp.transpose(stacked, (0, 3, 1, 2, 4))


def reference(vectors, links, momenta, directions):
    displaced = jnp.stack([displace(vectors, links, mu) for mu in range(3)], 0)
    xcoord = jnp.arange(LX, dtype=jnp.int32)[:, None]
    sites = jnp.arange(LY * LZ, dtype=jnp.int32)
    cosine, sine = phase_tables(momenta, xcoord, sites)
    full = elemental_block(vectors, displaced, cosine, sine)
    return jnp.take(full, directions, axis=1)
```

```python
import functools

import jax
import jax.numpy as jnp
from jax import lax
from jax.experimental import pallas as pl
from jax.experimental.pallas import tpu as pltpu
from jax.sharding import PartitionSpec as P

MESH = pl.DeviceIdType.MESH
F32 = jnp.float32
BF16 = jnp.bfloat16
VMEM = pl.BlockSpec(memory_space=pltpu.VMEM)
HBM = pl.BlockSpec(memory_space=pl.ANY)


def coords():
    s, k = lax.axis_index("space"), lax.axis_index("vec")
    return s // 4, (s // 2) % 2, s % 2, k // 4, k % 4


def lane_of(shape):
    return lax.broadcasted_iota(jnp.int32, shape, len(shape) - 1)


def exchange_kernel(x_ref, u_ref, v_ref, up_ref, dn_ref, lk_ref, ulo_ref,
                    stage, lstage, send, recv, lsend, lrecv, fsend, frecv, usend, urecv):
    y, xh, c, xl, z = coords()
    s, k = lax.axis_index("space"), lax.axis_index("vec")
    x = xh * 2 + xl
    selfish = c == xh
    q = 2 * y + c
    qn, qp = (q + 1) % 8, (q + 7) % 8
    s_next = (qn // 2 * 2 + xh) * 2 + qn % 2
    s_prev = (qp // 2 * 2 + xh) * 2 + qp % 2

    def target(i):
        xt, zt = (x + i // 4) % 4, (z + i % 4) % 4
        return (y * 2 + xt // 2) * 2 + xh, (xt % 2) * 4 + zt, xt * 4 + zt

    def origin(i):
        return (y * 2 + c) * 2 + i % 2, i // 2

    barrier = pltpu.get_barrier_semaphore()

    def greet(i, _):
        st, kt, _j = target(i)

        @pl.when(jnp.logical_or(st != s, kt != k))
        def _():
            pl.semaphore_signal(barrier, inc=1, device_id=(st, kt), device_id_type=MESH)

        so, ko = origin(i)

        @pl.when(jnp.logical_or(so != s, ko != k))
        def _():
            pl.semaphore_signal(barrier, inc=1, device_id=(so, ko), device_id_type=MESH)

        return 0

    lax.fori_loop(0, 16, greet, 0)
    pl.semaphore_signal(barrier, inc=1, device_id=(s_next, k), device_id_type=MESH)
    pl.semaphore_signal(barrier, inc=1, device_id=(s_prev, k), device_id_type=MESH)

    for xt in range(2):
        j = (xt * 2 + xl) * 4 + z
        lstage[xt, 48:56, :] = jnp.zeros((8, 128), F32)
        lstage[xt, 0:54, :] = u_ref[pl.ds(j, 54, stride=16), :]
    pl.semaphore_wait(barrier, jnp.where(selfish, 32, 34))

    def link_copy(xt):
        return pltpu.make_async_remote_copy(
            src_ref=lstage.at[xt], dst_ref=lk_ref.at[c], send_sem=lsend.at[xt],
            recv_sem=lrecv.at[c], device_id=((y * 2 + xt) * 2 + xh, k), device_id_type=MESH)

    for xt in range(2):
        mine = jnp.logical_and(selfish, xh == xt)

        @pl.when(mine)
        def _():
            pltpu.make_async_copy(lstage.at[xt], lk_ref.at[c], lrecv.at[c]).start()

        @pl.when(jnp.logical_not(mine))
        def _():
            link_copy(xt).start()

    lane = lane_of((144, 128))

    def main_copy(i):
        st, kt, j = target(i)
        return pltpu.make_async_remote_copy(
            src_ref=stage.at[i], dst_ref=v_ref.at[c, k], send_sem=send.at[i],
            recv_sem=recv.at[c * 8 + k], device_id=(st, kt), device_id_type=MESH)

    def put(i, _):
        st, kt, j = target(i)
        nxt = (j + 1) % 16
        stage[i, 0:288, :] = x_ref[pl.ds(j, 288, stride=16), :]
        re = x_ref[pl.ds(nxt, 144, stride=16), :]
        im = x_ref[pl.ds(144 * 16 + nxt, 144, stride=16), :]
        stage[i, 288:432, :] = jnp.where(lane < 64, re, pltpu.roll(im, 64, 1))
        mine = jnp.logical_and(st == s, kt == k)

        @pl.when(mine)
        def _():
            pltpu.make_async_copy(stage.at[i], v_ref.at[c, k], recv.at[c * 8 + k]).start()

        @pl.when(jnp.logical_not(mine))
        def _():
            main_copy(i).start()

        return 0

    lax.fori_loop(0, 16, put, 0)

    for p in range(2):
        pltpu.make_async_copy(lk_ref.at[p], lk_ref.at[p], lrecv.at[p]).wait()
    ulo = pltpu.make_async_remote_copy(
        src_ref=lk_ref.at[1, pl.ds(0, 24)], dst_ref=ulo_ref, send_sem=usend,
        recv_sem=urecv, device_id=(s_next, k), device_id_type=MESH)
    ulo.start()

    def hand(p, vb):
        return pltpu.make_async_remote_copy(
            src_ref=v_ref.at[p, vb, pl.ds(0, 288)],
            dst_ref=(up_ref if p == 0 else dn_ref).at[vb],
            send_sem=fsend.at[p, vb], recv_sem=frecv.at[p, vb],
            device_id=(s_prev if p == 0 else s_next, k), device_id_type=MESH)

    def pass_on(i, _):
        vb = (k // 4 * 4 + i // 4 * 4) % 8 + (z + 4 - i % 4) % 4
        for p in range(2):
            pltpu.make_async_copy(v_ref.at[p, vb], v_ref.at[p, vb], recv.at[p * 8 + vb]).wait()
            hand(p, vb).start()
        return 0

    lax.fori_loop(0, 8, pass_on, 0)

    def finish(i, _):
        for p in range(2):
            hand(p, i).wait_recv()
            hand(p, i).wait_send()
        return 0

    lax.fori_loop(0, 8, finish, 0)
    ulo.wait_recv()
    ulo.wait_send()
    for xt in range(2):

        @pl.when(jnp.logical_not(jnp.logical_and(selfish, xh == xt)))
        def _():
            link_copy(xt).wait_send()

    def sent(i, _):
        st, kt, _j = target(i)

        @pl.when(jnp.logical_or(st != s, kt != k))
        def _():
            main_copy(i).wait_send()

        return 0

    lax.fori_loop(0, 16, sent, 0)


def exchange(vectors, links):
    dma = pltpu.SemaphoreType.DMA
    return pl.pallas_call(
        exchange_kernel,
        out_shape=[
            jax.ShapeDtypeStruct((2, 8, 432, 128), F32),
            jax.ShapeDtypeStruct((8, 288, 128), F32),
            jax.ShapeDtypeStruct((8, 288, 128), F32),
            jax.ShapeDtypeStruct((2, 56, 128), F32),
            jax.ShapeDtypeStruct((24, 128), F32),
        ],
        in_specs=[VMEM, VMEM],
        out_specs=[HBM] * 5,
        scratch_shapes=[
            pltpu.VMEM((16, 432, 128), F32),
            pltpu.VMEM((2, 56, 128), F32),
            dma((16,)), dma((16,)), dma((2,)), dma((2,)),
            dma((2, 8)), dma((2, 8)), dma(()), dma(()),
        ],
        compiler_params=pltpu.CompilerParams(
            collective_id=0, has_side_effects=True, vmem_limit_bytes=24 << 20),
        name="exchange",
    )(vectors.reshape(288 * 16, 128), links.reshape(54 * 16, 128))


def halves(t):
    hi = t.astype(BF16)
    return hi, (t - hi.astype(F32)).astype(BF16)


def apply_link(link, field):
    out = []
    for i in range(3):
        re = im = None
        for j in range(3):
            ur, ui = link(i, j)
            fr, fi = field[j]
            a = ur * fr - ui * fi
            b = ur * fi + ui * fr
            re = a if re is None else re + a
            im = b if im is None else im + b
        out.append((re, im))
    return out


def products_kernel(mom_ref, v_ref, up_ref, dn_ref, lk_ref, ulo_ref, e_ref,
                    left, right, tab):
    y, xh, c, xl, z = coords()
    step = pl.program_id(0)
    m, mu = step // 3, step % 3

    @pl.when(step == 0)
    def _():
        line = (xh * 2 + xl) * 4 + z
        lane1 = lane_of((8, 128))
        low1 = lane1 < 64
        for mm in range(2):
            for place in range(3):
                plane = 4 * y + 2 * c + (jnp.where(low1, 0, 1) if place == 2 else place)
                row = 2 * line + (2 if place == 2 else jnp.where(low1, 0, 1))
                col = lane1 & 63
                n = (((mom_ref[mm, 0] * plane) & 15) * 4 + ((mom_ref[mm, 1] * row) & 31) * 2
                     + ((mom_ref[mm, 2] * col) & 63)) & 63
                theta = n.astype(F32) * (2.0 * jnp.pi / 64)
                tab[mm, place, 0] = jnp.cos(theta)
                tab[mm, place, 1] = jnp.sin(theta)

        rows = 16
        lane = lane_of((rows, 128))
        low = lane < 64
        col = lane & 63

        def group(g, _):
            vb, sub = g // 3, g % 3
            at = pl.multiple_of(g * rows, rows)

            def comp(ref, reim, col_, *lead):
                first = pl.multiple_of(reim * 144 + col_ * 48 + sub * rows, rows)
                return ref[(*lead, vb, pl.ds(first, rows), slice(None))]

            def link(ref, mu_, dagger, *lead):
                def get(i, j):
                    a, b = (j, i) if dagger else (i, j)
                    r = mu_ * 18 + a * 3 + b
                    ur = ref[(*lead, pl.ds(r, 1), slice(None))]
                    ui = ref[(*lead, pl.ds(r + 9, 1), slice(None))]
                    return ur, (-ui if dagger else ui)
                return get

            def put_right(mu_, place, cc, dr, di):
                kk = pl.ds((6 + cc if place == 2 else cc * 2 + place) * 128, 128)
                for i, t in enumerate((dr, di - dr, dr + di)):
                    hi, lo = halves(t)
                    right[mu_, i, 0, pl.ds(at, rows), kk] = hi
                    right[mu_, i, 1, pl.ds(at, rows), kk] = lo

            v = [[(comp(v_ref, 0, cc, p), comp(v_ref, 1, cc, p)) for cc in range(3)] for p in range(2)]
            above = [(comp(up_ref, 0, cc), comp(up_ref, 1, cc)) for cc in range(3)]
            below = [(comp(dn_ref, 0, cc), comp(dn_ref, 1, cc)) for cc in range(3)]
            packed = []
            for p in range(2):
                packed.append([
                    v_ref[p, vb, pl.ds(pl.multiple_of(288 + cc * 48 + sub * rows, rows), rows), :]
                    for cc in range(3)])
            ext = [
                (jnp.where(low, packed[0][cc], pltpu.roll(packed[1][cc], 64, 1)),
                 jnp.where(low, pltpu.roll(packed[0][cc], 64, 1), packed[1][cc]))
                for cc in range(3)]

            for mm in range(2):
                for place in range(3):
                    co, si = tab[mm, place, 0, 0:1], tab[mm, place, 1, 0:1]
                    for cc in range(3):
                        vr, vi = ext[cc] if place == 2 else v[place][cc]
                        lr = vr * co - vi * si
                        li = -(vr * si + vi * co)
                        kk = pl.ds((6 + cc if place == 2 else cc * 2 + place) * 128, 128)
                        for i, t in enumerate((lr + li, lr, li)):
                            hi, lo = halves(t)
                            left[mm, i, 0, pl.ds(at, rows), kk] = hi
                            left[mm, i, 1, pl.ds(at, rows), kk] = lo

            spill = []
            for p in range(2):
                fwd = apply_link(link(lk_ref, 0, False, p), v[1] if p == 0 else above)
                bwd = (apply_link(link(ulo_ref, 0, True), below) if p == 0
                       else apply_link(link(lk_ref, 0, True, 0), v[0]))
                for cc in range(3):
                    put_right(0, p, cc, fwd[cc][0] - bwd[cc][0], fwd[cc][1] - bwd[cc][1])
                shifted = []
                for cc in range(3):
                    vr, vi = v[p][cc]
                    shifted.append((
                        pltpu.roll(jnp.where(low, packed[p][cc], vr), 64, 1),
                        jnp.where(low, pltpu.roll(vi, 64, 1), packed[p][cc])))
                fwd = apply_link(link(lk_ref, 1, False, p), shifted)
                bwd = apply_link(link(lk_ref, 1, True, p), v[p])
                turned = []
                for cc in range(3):
                    tr, ti = pltpu.roll(bwd[cc][0], 64, 1), pltpu.roll(bwd[cc][1], 64, 1)
                    turned.append((tr, ti))
                    put_right(1, p, cc, fwd[cc][0] - jnp.where(low, 0.0, tr),
                              fwd[cc][1] - jnp.where(low, 0.0, ti))
                spill.append((bwd, turned))
                def ahead(t):
                    return jnp.where(col == 63, pltpu.roll(t, 63, 1), pltpu.roll(t, 127, 1))

                def behind(t):
                    return jnp.where(col == 0, pltpu.roll(t, 65, 1), pltpu.roll(t, 1, 1))

                fwd = apply_link(link(lk_ref, 2, False, p), [(ahead(a), ahead(b)) for a, b in v[p]])
                bwd = apply_link(link(lk_ref, 2, True, p), v[p])
                for cc in range(3):
                    put_right(2, p, cc, fwd[cc][0] - behind(bwd[cc][0]),
                              fwd[cc][1] - behind(bwd[cc][1]))
            for cc in range(3):
                put_right(1, 2, cc,
                          -jnp.where(low, spill[0][1][cc][0], spill[1][0][cc][0]),
                          -jnp.where(low, spill[0][1][cc][1], spill[1][0][cc][1]))
            return 0

        lax.fori_loop(0, 24, group, 0)

    def product(depth):
        dims = (((1,), (1,)), ((), ()))

        def one(i):
            d = pl.ds(0, depth)
            lh, ll = left[m, i, 0, :, d], left[m, i, 1, :, d]
            rh, rl = right[mu, i, 0, :, d], right[mu, i, 1, :, d]
            dot = functools.partial(lax.dot_general, dimension_numbers=dims, preferred_element_type=F32)
            return dot(lh, rh) + dot(lh, rl) + dot(ll, rh)

        k1 = one(0)
        e_ref[0, 1] = k1 + one(1)
        e_ref[0, 0] = k1 - one(2)

    @pl.when(mu == 1)
    def _():
        product(1152)

    @pl.when(mu != 1)
    def _():
        product(768)


def products(momenta, v, up, dn, lk, ulo):
    once = pl.Buffered(1)
    whole = lambda a: pl.BlockSpec(a.shape, lambda i: (0,) * a.ndim, pipeline_mode=once)
    return pl.pallas_call(
        products_kernel,
        grid=(6,),
        out_shape=jax.ShapeDtypeStruct((6, 2, 384, 384), F32),
        in_specs=[pl.BlockSpec(memory_space=pltpu.SMEM)] + [whole(a) for a in (v, up, dn, lk, ulo)],
        out_specs=pl.BlockSpec((1, 2, 384, 384), lambda i: (i, 0, 0, 0)),
        scratch_shapes=[
            pltpu.VMEM((2, 3, 2, 384, 1152), BF16),
            pltpu.VMEM((3, 3, 2, 384, 1152), BF16),
            pltpu.VMEM((2, 3, 2, 8, 128), F32),
        ],
        compiler_params=pltpu.CompilerParams(vmem_limit_bytes=56 << 20),
        cost_estimate=pl.CostEstimate(flops=2 * 18 * 3 * 384 * 384 * 896, bytes_accessed=13 << 20, transcendentals=0),
        name="products",
    )(momenta, v, up, dn, lk, ulo)


def sums_kernel(e_ref, out_ref, cin, cs, yin, ys, xin, xs, zst, zin, zs, lin,
                csend, crecv, asend, arecv, bsend, brecv, zsend, zrecv, lsend, lrecv):
    y, xh, c, xl, z = coords()
    s, k = lax.axis_index("space"), lax.axis_index("vec")
    x = xh * 2 + xl

    def dev(y_, x_, c_, z_):
        return (y_ * 2 + x_ // 2) * 2 + c_, (x_ % 2) * 4 + z_

    def on_y(d):
        return dev((y + d) % 4, x, c, z)

    def on_x(d):
        return dev(y, (x + d) % 4, c, z)

    def on_z(d):
        return dev(y, x, c, (z + d) % 4)

    partner = dev(y, x, 1 - c, z)
    twin = dev(y, xh * 2 + 1 - xl, c, z)
    barrier = pltpu.get_barrier_semaphore()
    pl.semaphore_signal(barrier, inc=1, device_id=partner, device_id_type=MESH)
    for d in (1, 2, 3):
        for on in (on_y, on_x, on_z):
            pl.semaphore_signal(barrier, inc=1, device_id=on(d), device_id_type=MESH)
    pl.semaphore_wait(barrier, 10)

    def core_copy(b):
        return pltpu.make_async_remote_copy(
            src_ref=e_ref.at[b, :, :, 1 - c], dst_ref=cin.at[b], send_sem=csend.at[b],
            recv_sem=crecv.at[b], device_id=partner, device_id_type=MESH)

    for b in range(6):
        core_copy(b).start()

    def first(b, d):
        if b % 2 == 0:
            yt = (y + d) % 4
            src, to = cs.at[b, :, yt], on_y(d)
            dst = yin.at[b // 2, d - 1]
        else:
            xt = (x + d) % 4
            src, to = cs.at[b, xt % 2, :, xt // 2], on_x(d)
            dst = xin.at[b // 2, d - 1]
        return pltpu.make_async_remote_copy(
            src_ref=src, dst_ref=dst, send_sem=asend.at[b, d - 1],
            recv_sem=arecv.at[b, d - 1], device_id=to, device_id_type=MESH)

    def second(b, d):
        if b % 2 == 0:
            xt = (x + d) % 4
            src, to = ys.at[b // 2, xt % 2, xt // 2], on_x(d)
        else:
            src, to = xs.at[b // 2, (y + d) % 4], on_y(d)
        return pltpu.make_async_remote_copy(
            src_ref=src, dst_ref=lin.at[b, d - 1], send_sem=bsend.at[b, d - 1],
            recv_sem=brecv.at[b, d - 1], device_id=to, device_id_type=MESH)

    def third(d):
        return pltpu.make_async_remote_copy(
            src_ref=zst.at[d], dst_ref=zin.at[d - 1], send_sem=zsend.at[d - 1],
            recv_sem=zrecv.at[d - 1], device_id=on_z(d), device_id_type=MESH)

    last = pltpu.make_async_remote_copy(
        src_ref=zs.at[0], dst_ref=zs.at[1], send_sem=lsend, recv_sem=lrecv,
        device_id=twin, device_id_type=MESH)

    for b in range(6):
        core_copy(b).wait_recv()
        for ri in range(2):
            def add(i, _):
                cs[b, ri, i // 2, i % 2] = e_ref[b, ri, i, c] + cin[b, ri, i]
                return 0
            lax.fori_loop(0, 8, add, 0)
        for d in (1, 2, 3):
            first(b, d).start()

    for b in range(6):
        for d in (1, 2, 3):
            first(b, d).wait_recv()
        if b % 2 == 0:
            for ri in range(2):
                for h in range(2):
                    ys[b // 2, ri, h] = (cs[b, ri, y, h] + yin[b // 2, 0, ri, h]) + (
                        yin[b // 2, 1, ri, h] + yin[b // 2, 2, ri, h])
        else:
            for i in range(4):
                xs[b // 2, i] = (cs[b, xl, i, xh] + xin[b // 2, 0, i]) + (
                    xin[b // 2, 1, i] + xin[b // 2, 2, i])
        for d in (1, 2, 3):
            second(b, d).start()

    for b in range(6):
        for d in (1, 2, 3):
            second(b, d).wait_recv()
        own = ys[b // 2, xl, xh] if b % 2 == 0 else xs[b // 2, y]
        t = (own + lin[b, 0]) + (lin[b, 1] + lin[b, 2])
        for d in range(4):
            zt = (z + d) % 4
            zst[d, b] = jnp.where(
                lane_of((24, 128)) < 48,
                pltpu.roll(t, (384 - 48 * zt) % 384, 1)[:, 0:128],
                pltpu.roll(t, (624 - 48 * zt) % 384, 1)[:, 0:128])
    for d in (1, 2, 3):
        third(d).start()
    for d in (1, 2, 3):
        third(d).wait_recv()
    zs[0] = (zst[0] + zin[0]) + (zin[1] + zin[2])
    last.start()
    last.wait_recv()
    for b in range(6):
        own = pltpu.roll(zs[0, b], (128 - 48 * xl) % 128, 1)[:, 0:48]
        other = pltpu.roll(zs[1, b], (128 - 48 * xl) % 128, 1)[:, 0:48]
        out_ref[b, xl] = own
        out_ref[b, 1 - xl] = other
    last.wait_send()
    for d in (1, 2, 3):
        third(d).wait_send()
    for b in range(6):
        core_copy(b).wait_send()
        for d in (1, 2, 3):
            first(b, d).wait_send()
            second(b, d).wait_send()


def sums(e):
    dma = pltpu.SemaphoreType.DMA
    return pl.pallas_call(
        sums_kernel,
        out_shape=jax.ShapeDtypeStruct((6, 2, 24, 48), F32),
        in_specs=[VMEM],
        out_specs=VMEM,
        scratch_shapes=[
            pltpu.VMEM((6, 2, 8, 24, 384), F32),
            pltpu.VMEM((6, 2, 4, 2, 24, 384), F32),
            pltpu.VMEM((3, 3, 2, 2, 24, 384), F32),
            pltpu.VMEM((3, 2, 2, 24, 384), F32),
            pltpu.VMEM((3, 3, 4, 24, 384), F32),
            pltpu.VMEM((3, 4, 24, 384), F32),
            pltpu.VMEM((4, 6, 24, 128), F32),
            pltpu.VMEM((3, 6, 24, 128), F32),
            pltpu.VMEM((2, 6, 24, 128), F32),
            pltpu.VMEM((6, 3, 24, 384), F32),
            dma((6,)), dma((6,)), dma((6, 3)), dma((6, 3)), dma((6, 3)), dma((6, 3)),
            dma((3,)), dma((3,)), dma(()), dma(()),
        ],
        compiler_params=pltpu.CompilerParams(
            collective_id=1, has_side_effects=True, vmem_limit_bytes=48 << 20),
        name="sums",
    )(e.reshape(6, 2, 8, 2, 24, 384))


def on_device(vectors, links, momenta, directions):
    e = products(momenta, *exchange(vectors, links))
    out = sums(e).reshape(2, 3, 2, 24, 48)
    picked = []
    for n in range(3):
        d = directions[n]
        picked.append(jnp.where(d == 0, out[:, 0], jnp.where(d == 1, out[:, 1], out[:, 2])))
    return jnp.stack(picked, axis=1)


def solution(mesh):
    placed = (
        P(None, None, "vec", "space", None),
        P(None, None, None, None, "space", None),
        P(),
        P(),
    )
    return jax.shard_map(
        on_device,
        mesh=mesh,
        in_specs=placed,
        out_specs=P(None, None, None, "space", "vec"),
        check_vma=False,
    )
```

```python
import functools

import jax
import jax.numpy as jnp
from jax import lax
from jax.experimental import pallas as pl
from jax.experimental.pallas import tpu as pltpu
from jax.sharding import PartitionSpec as P

MESH = pl.DeviceIdType.MESH
F32 = jnp.float32
BF16 = jnp.bfloat16
VMEM = pl.BlockSpec(memory_space=pltpu.VMEM)
HBM = pl.BlockSpec(memory_space=pl.ANY)


def coords():
    s, k = lax.axis_index("space"), lax.axis_index("vec")
    return s // 4, (s // 2) % 2, s % 2, k // 4, k % 4


def lane_of(shape):
    return lax.broadcasted_iota(jnp.int32, shape, len(shape) - 1)


STEPS = ((2, 2), (1, 2), (3, 2), (2, 1), (2, 3), (1, 1), (3, 3), (1, 3),
         (3, 1), (2, 0), (0, 2), (0, 1), (0, 3), (1, 0), (3, 0), (0, 0))


def exchange_kernel(x_ref, u_ref, v_ref, up_ref, dn_ref, lk_ref, ulo_ref,
                    stage, lstage, send, recv, lsend, lrecv, fsend, frecv, usend, urecv):
    y, xh, c, xl, z = coords()
    s, k = lax.axis_index("space"), lax.axis_index("vec")
    x = xh * 2 + xl
    selfish = c == xh
    q = 2 * y + c
    qn, qp = (q + 1) % 8, (q + 7) % 8
    s_next = (qn // 2 * 2 + xh) * 2 + qn % 2
    s_prev = (qp // 2 * 2 + xh) * 2 + qp % 2

    def target(i):
        xt, zt = (x + STEPS[i][0]) % 4, (z + STEPS[i][1]) % 4
        return (y * 2 + xt // 2) * 2 + xh, (xt % 2) * 4 + zt, xt * 4 + zt

    def origin(i):
        return (y * 2 + c) * 2 + i % 2, i // 2

    barrier = pltpu.get_barrier_semaphore()

    def greet(i):
        st, kt, _j = target(i)

        @pl.when(jnp.logical_or(st != s, kt != k))
        def _():
            pl.semaphore_signal(barrier, inc=1, device_id=(st, kt), device_id_type=MESH)

        so, ko = origin(i)

        @pl.when(jnp.logical_or(so != s, ko != k))
        def _():
            pl.semaphore_signal(barrier, inc=1, device_id=(so, ko), device_id_type=MESH)

    for i in range(16):
        greet(i)
    pl.semaphore_signal(barrier, inc=1, device_id=(s_next, k), device_id_type=MESH)
    pl.semaphore_signal(barrier, inc=1, device_id=(s_prev, k), device_id_type=MESH)

    for xt in range(2):
        j = (xt * 2 + xl) * 4 + z
        lstage[xt, 48:56, :] = jnp.zeros((8, 128), F32)
        lstage[xt, 0:54, :] = u_ref[pl.ds(j, 54, stride=16), :]
    pl.semaphore_wait(barrier, jnp.where(selfish, 32, 34))

    def link_copy(xt):
        return pltpu.make_async_remote_copy(
            src_ref=lstage.at[xt], dst_ref=lk_ref.at[c], send_sem=lsend.at[xt],
            recv_sem=lrecv.at[c], device_id=((y * 2 + xt) * 2 + xh, k), device_id_type=MESH)

    for xt in range(2):
        mine = jnp.logical_and(selfish, xh == xt)

        @pl.when(mine)
        def _():
            pltpu.make_async_copy(lstage.at[xt], lk_ref.at[c], lrecv.at[c]).start()

        @pl.when(jnp.logical_not(mine))
        def _():
            link_copy(xt).start()

    lane = lane_of((144, 128))

    def main_copy(i):
        st, kt, j = target(i)
        return pltpu.make_async_remote_copy(
            src_ref=stage.at[i], dst_ref=v_ref.at[c, k], send_sem=send.at[i],
            recv_sem=recv.at[c * 8 + k], device_id=(st, kt), device_id_type=MESH)

    def put(i):
        st, kt, j = target(i)
        nxt = (j + 1) % 16
        stage[i, 0:288, :] = x_ref[pl.ds(j, 288, stride=16), :]
        re = x_ref[pl.ds(nxt, 144, stride=16), :]
        im = x_ref[pl.ds(144 * 16 + nxt, 144, stride=16), :]
        stage[i, 288:432, :] = jnp.where(lane < 64, re, pltpu.roll(im, 64, 1))
        mine = jnp.logical_and(st == s, kt == k)

        @pl.when(mine)
        def _():
            pltpu.make_async_copy(stage.at[i], v_ref.at[c, k], recv.at[c * 8 + k]).start()

        @pl.when(jnp.logical_not(mine))
        def _():
            main_copy(i).start()

    for i in range(16):
        put(i)

    for p in range(2):
        pltpu.make_async_copy(lk_ref.at[p], lk_ref.at[p], lrecv.at[p]).wait()
    ulo = pltpu.make_async_remote_copy(
        src_ref=lk_ref.at[1, pl.ds(0, 24)], dst_ref=ulo_ref, send_sem=usend,
        recv_sem=urecv, device_id=(s_next, k), device_id_type=MESH)
    ulo.start()

    def hand(p, vb):
        return pltpu.make_async_remote_copy(
            src_ref=v_ref.at[p, vb, pl.ds(0, 288)],
            dst_ref=(up_ref if p == 0 else dn_ref).at[vb],
            send_sem=fsend.at[p, vb], recv_sem=frecv.at[p, vb],
            device_id=(s_prev if p == 0 else s_next, k), device_id_type=MESH)

    def pass_on(i):
        xs, zs = (x + 4 - STEPS[i][0]) % 4, (z + 4 - STEPS[i][1]) % 4
        vb = (xs % 2) * 4 + zs

        @pl.when(xs // 2 == c)
        def _():
            for p in range(2):
                pltpu.make_async_copy(v_ref.at[p, vb], v_ref.at[p, vb], recv.at[p * 8 + vb]).wait()
                hand(p, vb).start()

    for i in range(16):
        pass_on(i)

    def finish(i, _):
        for p in range(2):
            hand(p, i).wait_recv()
            hand(p, i).wait_send()
        return 0

    lax.fori_loop(0, 8, finish, 0)
    ulo.wait_recv()
    ulo.wait_send()
    for xt in range(2):

        @pl.when(jnp.logical_not(jnp.logical_and(selfish, xh == xt)))
        def _():
            link_copy(xt).wait_send()

    def sent(i):
        st, kt, _j = target(i)

        @pl.when(jnp.logical_or(st != s, kt != k))
        def _():
            main_copy(i).wait_send()

    for i in range(16):
        sent(i)


def exchange(vectors, links):
    dma = pltpu.SemaphoreType.DMA
    return pl.pallas_call(
        exchange_kernel,
        out_shape=[
            jax.ShapeDtypeStruct((2, 8, 432, 128), F32),
            jax.ShapeDtypeStruct((8, 288, 128), F32),
            jax.ShapeDtypeStruct((8, 288, 128), F32),
            jax.ShapeDtypeStruct((2, 56, 128), F32),
            jax.ShapeDtypeStruct((24, 128), F32),
        ],
        in_specs=[VMEM, VMEM],
        out_specs=[HBM] * 5,
        scratch_shapes=[
            pltpu.VMEM((16, 432, 128), F32),
            pltpu.VMEM((2, 56, 128), F32),
            dma((16,)), dma((16,)), dma((2,)), dma((2,)),
            dma((2, 8)), dma((2, 8)), dma(()), dma(()),
        ],
        compiler_params=pltpu.CompilerParams(
            collective_id=0, has_side_effects=True, vmem_limit_bytes=24 << 20),
        name="exchange",
    )(vectors.reshape(288 * 16, 128), links.reshape(54 * 16, 128))


def halves(t):
    hi = t.astype(BF16)
    return hi, (t - hi.astype(F32)).astype(BF16)


def apply_link(link, field):
    out = []
    for i in range(3):
        re = im = None
        for j in range(3):
            ur, ui = link(i, j)
            fr, fi = field[j]
            a = ur * fr - ui * fi
            b = ur * fi + ui * fr
            re = a if re is None else re + a
            im = b if im is None else im + b
        out.append((re, im))
    return out


def elementals_kernel(mom_ref, v_ref, up_ref, dn_ref, lk_ref, ulo_ref, out_ref,
                      left, right, tab, e_ref, cin, cs, yin, ys, xin, xs, zst, zin, zs, lin,
                      csend, crecv, asend, arecv, bsend, brecv, zsend, zrecv, lsend, lrecv):
    y, xh, c, xl, z = coords()
    x = xh * 2 + xl

    def dev(y_, x_, c_, z_):
        return (y_ * 2 + x_ // 2) * 2 + c_, (x_ % 2) * 4 + z_

    def on_y(d):
        return dev((y + d) % 4, x, c, z)

    def on_x(d):
        return dev(y, (x + d) % 4, c, z)

    def on_z(d):
        return dev(y, x, c, (z + d) % 4)

    partner = dev(y, x, 1 - c, z)
    twin = dev(y, xh * 2 + 1 - xl, c, z)
    barrier = pltpu.get_barrier_semaphore()
    pl.semaphore_signal(barrier, inc=1, device_id=partner, device_id_type=MESH)
    for d in (1, 2, 3):
        for on in (on_y, on_x, on_z):
            pl.semaphore_signal(barrier, inc=1, device_id=on(d), device_id_type=MESH)

    line = (xh * 2 + xl) * 4 + z
    lane1 = lane_of((8, 128))
    low1 = lane1 < 64
    for mm in range(2):
        for place in range(3):
            plane = 4 * y + 2 * c + (jnp.where(low1, 0, 1) if place == 2 else place)
            row = 2 * line + (2 if place == 2 else jnp.where(low1, 0, 1))
            col = lane1 & 63
            n = (((mom_ref[mm, 0] * plane) & 15) * 4 + ((mom_ref[mm, 1] * row) & 31) * 2
                 + ((mom_ref[mm, 2] * col) & 63)) & 63
            theta = n.astype(F32) * (2.0 * jnp.pi / 64)
            tab[mm, place, 0] = jnp.cos(theta)
            tab[mm, place, 1] = jnp.sin(theta)

    rows = 16
    lane = lane_of((rows, 128))
    low = lane < 64
    col = lane & 63

    def group(g, _):
        vb, sub = g // 3, g % 3
        at = pl.multiple_of(g * rows, rows)

        def comp(ref, reim, col_, *lead):
            first = pl.multiple_of(reim * 144 + col_ * 48 + sub * rows, rows)
            return ref[(*lead, vb, pl.ds(first, rows), slice(None))]

        def link(ref, mu_, dagger, *lead):
            def get(i, j):
                a, b = (j, i) if dagger else (i, j)
                r = mu_ * 18 + a * 3 + b
                ur = ref[(*lead, pl.ds(r, 1), slice(None))]
                ui = ref[(*lead, pl.ds(r + 9, 1), slice(None))]
                return ur, (-ui if dagger else ui)
            return get

        def put_right(mu_, place, cc, dr, di):
            kk = pl.ds((6 + cc if place == 2 else cc * 2 + place) * 128, 128)
            for i, t in enumerate((dr, di - dr, dr + di)):
                hi, lo = halves(t)
                right[mu_, i, 0, pl.ds(at, rows), kk] = hi
                right[mu_, i, 1, pl.ds(at, rows), kk] = lo

        v = [[(comp(v_ref, 0, cc, p), comp(v_ref, 1, cc, p)) for cc in range(3)] for p in range(2)]
        above = [(comp(up_ref, 0, cc), comp(up_ref, 1, cc)) for cc in range(3)]
        below = [(comp(dn_ref, 0, cc), comp(dn_ref, 1, cc)) for cc in range(3)]
        packed = []
        for p in range(2):
            packed.append([
                v_ref[p, vb, pl.ds(pl.multiple_of(288 + cc * 48 + sub * rows, rows), rows), :]
                for cc in range(3)])
        ext = [
            (jnp.where(low, packed[0][cc], pltpu.roll(packed[1][cc], 64, 1)),
             jnp.where(low, pltpu.roll(packed[0][cc], 64, 1), packed[1][cc]))
            for cc in range(3)]

        for mm in range(2):
            for place in range(3):
                co, si = tab[mm, place, 0, 0:1], tab[mm, place, 1, 0:1]
                for cc in range(3):
                    vr, vi = ext[cc] if place == 2 else v[place][cc]
                    lr = vr * co - vi * si
                    li = -(vr * si + vi * co)
                    kk = pl.ds((6 + cc if place == 2 else cc * 2 + place) * 128, 128)
                    for i, t in enumerate((lr + li, lr, li)):
                        hi, lo = halves(t)
                        left[mm, i, 0, pl.ds(at, rows), kk] = hi
                        left[mm, i, 1, pl.ds(at, rows), kk] = lo

        spill = []
        for p in range(2):
            fwd = apply_link(link(lk_ref, 0, False, p), v[1] if p == 0 else above)
            bwd = (apply_link(link(ulo_ref, 0, True), below) if p == 0
                   else apply_link(link(lk_ref, 0, True, 0), v[0]))
            for cc in range(3):
                put_right(0, p, cc, fwd[cc][0] - bwd[cc][0], fwd[cc][1] - bwd[cc][1])
            shifted = []
            for cc in range(3):
                vr, vi = v[p][cc]
                shifted.append((
                    pltpu.roll(jnp.where(low, packed[p][cc], vr), 64, 1),
                    jnp.where(low, pltpu.roll(vi, 64, 1), packed[p][cc])))
            fwd = apply_link(link(lk_ref, 1, False, p), shifted)
            bwd = apply_link(link(lk_ref, 1, True, p), v[p])
            turned = []
            for cc in range(3):
                tr, ti = pltpu.roll(bwd[cc][0], 64, 1), pltpu.roll(bwd[cc][1], 64, 1)
                turned.append((tr, ti))
                put_right(1, p, cc, fwd[cc][0] - jnp.where(low, 0.0, tr),
                          fwd[cc][1] - jnp.where(low, 0.0, ti))
            spill.append((bwd, turned))
            def ahead(t):
                return jnp.where(col == 63, pltpu.roll(t, 63, 1), pltpu.roll(t, 127, 1))

            def behind(t):
                return jnp.where(col == 0, pltpu.roll(t, 65, 1), pltpu.roll(t, 1, 1))

            fwd = apply_link(link(lk_ref, 2, False, p), [(ahead(a), ahead(b)) for a, b in v[p]])
            bwd = apply_link(link(lk_ref, 2, True, p), v[p])
            for cc in range(3):
                put_right(2, p, cc, fwd[cc][0] - behind(bwd[cc][0]),
                          fwd[cc][1] - behind(bwd[cc][1]))
        for cc in range(3):
            put_right(1, 2, cc,
                      -jnp.where(low, spill[0][1][cc][0], spill[1][0][cc][0]),
                      -jnp.where(low, spill[0][1][cc][1], spill[1][0][cc][1]))
        return 0

    lax.fori_loop(0, 24, group, 0)


    pl.semaphore_wait(barrier, 10)

    def product(b, depth):
        m, mu = b // 3, b % 3
        dims = (((1,), (1,)), ((), ()))

        def one(i):
            d = pl.ds(0, depth)
            lh, ll = left[m, i, 0, :, d], left[m, i, 1, :, d]
            rh, rl = right[mu, i, 0, :, d], right[mu, i, 1, :, d]
            dot = functools.partial(lax.dot_general, dimension_numbers=dims, preferred_element_type=F32)
            return (dot(lh, rh) + dot(lh, rl) + dot(ll, rh)).reshape(8, 2, 24, 384)

        k1 = one(0)
        e_ref[b, 1] = k1 + one(1)
        e_ref[b, 0] = k1 - one(2)

    def core_copy(b):
        return pltpu.make_async_remote_copy(
            src_ref=e_ref.at[b, :, :, 1 - c], dst_ref=cin.at[b], send_sem=csend.at[b],
            recv_sem=crecv.at[b], device_id=partner, device_id_type=MESH)

    def first(b, d, even):
        if even:
            src, to = cs.at[b, :, (y + d) % 4], on_y(d)
            dst = yin.at[b // 2, d - 1]
        else:
            xt = (x + d) % 4
            src, to = cs.at[b, xt % 2, :, xt // 2], on_x(d)
            dst = xin.at[b // 2, d - 1]
        return pltpu.make_async_remote_copy(
            src_ref=src, dst_ref=dst, send_sem=asend.at[b, d - 1],
            recv_sem=arecv.at[b, d - 1], device_id=to, device_id_type=MESH)

    def second(b, d, even):
        if even:
            xt = (x + d) % 4
            src, to = ys.at[b // 2, xt % 2, xt // 2], on_x(d)
        else:
            src, to = xs.at[b // 2, (y + d) % 4], on_y(d)
        return pltpu.make_async_remote_copy(
            src_ref=src, dst_ref=lin.at[b, d - 1], send_sem=bsend.at[b, d - 1],
            recv_sem=brecv.at[b, d - 1], device_id=to, device_id_type=MESH)

    def third(d):
        return pltpu.make_async_remote_copy(
            src_ref=zst.at[d], dst_ref=zin.at[d - 1], send_sem=zsend.at[d - 1],
            recv_sem=zrecv.at[d - 1], device_id=on_z(d), device_id_type=MESH)

    last = pltpu.make_async_remote_copy(
        src_ref=zs.at[0], dst_ref=zs.at[1], send_sem=lsend, recv_sem=lrecv,
        device_id=twin, device_id_type=MESH)

    def by_order(b, act):
        @pl.when(b % 2 == 0)
        def _():
            act(True)

        @pl.when(b % 2 == 1)
        def _():
            act(False)

    def over_core(b):
        core_copy(b).wait_recv()
        for i in range(8):
            for ri in range(2):
                cs[b, ri, i // 2, i % 2] = e_ref[b, ri, i, c] + cin[b, ri, i]

        def go(even):
            for d in (1, 2, 3):
                first(b, d, even).start()

        by_order(b, go)

    def over_first(b):
        h = b // 2

        def go(even):
            for d in (1, 2, 3):
                first(b, d, even).wait_recv()
            if even:
                for ri in range(2):
                    for g in range(2):
                        ys[h, ri, g] = (cs[b, ri, y, g] + yin[h, 0, ri, g]) + (
                            yin[h, 1, ri, g] + yin[h, 2, ri, g])
            else:
                for i in range(4):
                    xs[h, i] = (cs[b, xl, i, xh] + xin[h, 0, i]) + (xin[h, 1, i] + xin[h, 2, i])
            for d in (1, 2, 3):
                second(b, d, even).start()

        by_order(b, go)

    def over_second(b):
        def go(even):
            for d in (1, 2, 3):
                second(b, d, even).wait_recv()
            own = ys[b // 2, xl, xh] if even else xs[b // 2, y]
            t = (own + lin[b, 0]) + (lin[b, 1] + lin[b, 2])
            for d in range(4):
                zt = (z + d) % 4
                zst[d, b] = jnp.where(
                    lane_of((24, 128)) < 48,
                    pltpu.roll(t, (384 - 48 * zt) % 384, 1)[:, 0:128],
                    pltpu.roll(t, (624 - 48 * zt) % 384, 1)[:, 0:128])

        by_order(b, go)

    def turn(t, _):
        @pl.when(t < 6)
        def _():
            @pl.when(t % 3 == 1)
            def _():
                product(t, 1152)

            @pl.when(t % 3 != 1)
            def _():
                product(t, 768)

            core_copy(t).start()

        @pl.when(jnp.logical_and(t >= 1, t < 7))
        def _():
            over_core(t - 1)

        @pl.when(jnp.logical_and(t >= 3, t < 9))
        def _():
            over_first(t - 3)

        @pl.when(t >= 4)
        def _():
            over_second(t - 4)

        return 0

    lax.fori_loop(0, 10, turn, 0)

    for d in (1, 2, 3):
        third(d).start()
    for d in (1, 2, 3):
        third(d).wait_recv()
    zs[0] = (zst[0] + zin[0]) + (zin[1] + zin[2])
    last.start()
    last.wait_recv()
    for b in range(6):
        own = pltpu.roll(zs[0, b], (128 - 48 * xl) % 128, 1)[:, 0:48]
        other = pltpu.roll(zs[1, b], (128 - 48 * xl) % 128, 1)[:, 0:48]
        out_ref[b, xl] = own
        out_ref[b, 1 - xl] = other
    last.wait_send()
    for d in (1, 2, 3):
        third(d).wait_send()

    def sent(b, _):
        core_copy(b).wait_send()

        def go(even):
            for d in (1, 2, 3):
                first(b, d, even).wait_send()
                second(b, d, even).wait_send()

        by_order(b, go)
        return 0

    lax.fori_loop(0, 6, sent, 0)


def elementals(momenta, v, up, dn, lk, ulo):
    dma = pltpu.SemaphoreType.DMA
    return pl.pallas_call(
        elementals_kernel,
        out_shape=jax.ShapeDtypeStruct((6, 2, 24, 48), F32),
        in_specs=[pl.BlockSpec(memory_space=pltpu.SMEM)] + [VMEM] * 5,
        out_specs=VMEM,
        scratch_shapes=[
            pltpu.VMEM((2, 3, 2, 384, 1152), BF16),
            pltpu.VMEM((3, 3, 2, 384, 1152), BF16),
            pltpu.VMEM((2, 3, 2, 8, 128), F32),
            pltpu.VMEM((6, 2, 8, 2, 24, 384), F32),
            pltpu.VMEM((6, 2, 8, 24, 384), F32),
            pltpu.VMEM((6, 2, 4, 2, 24, 384), F32),
            pltpu.VMEM((3, 3, 2, 2, 24, 384), F32),
            pltpu.VMEM((3, 2, 2, 24, 384), F32),
            pltpu.VMEM((3, 3, 4, 24, 384), F32),
            pltpu.VMEM((3, 4, 24, 384), F32),
            pltpu.VMEM((4, 6, 24, 128), F32),
            pltpu.VMEM((3, 6, 24, 128), F32),
            pltpu.VMEM((2, 6, 24, 128), F32),
            pltpu.VMEM((6, 3, 24, 384), F32),
            dma((6,)), dma((6,)), dma((6, 3)), dma((6, 3)), dma((6, 3)), dma((6, 3)),
            dma((3,)), dma((3,)), dma(()), dma(()),
        ],
        compiler_params=pltpu.CompilerParams(
            collective_id=1, has_side_effects=True, vmem_limit_bytes=54 << 20),
        cost_estimate=pl.CostEstimate(flops=2 * 18 * 3 * 384 * 384 * 896, bytes_accessed=6 << 20, transcendentals=0),
        name="elementals",
    )(momenta, v, up, dn, lk, ulo)


def on_device(vectors, links, momenta, directions):
    out = elementals(momenta, *exchange(vectors, links)).reshape(2, 3, 2, 24, 48)
    picked = []
    for n in range(3):
        d = directions[n]
        picked.append(jnp.where(d == 0, out[:, 0], jnp.where(d == 1, out[:, 1], out[:, 2])))
    return jnp.stack(picked, axis=1)


def solution(mesh):
    placed = (
        P(None, None, "vec", "space", None),
        P(None, None, None, None, "space", None),
        P(),
        P(),
    )
    return jax.shard_map(
        on_device,
        mesh=mesh,
        in_specs=placed,
        out_specs=P(None, None, None, "space", "vec"),
        check_vma=False,
    )
```

```python
import functools

import jax
import jax.numpy as jnp
from jax import lax
from jax.experimental import pallas as pl
from jax.experimental.pallas import tpu as pltpu
from jax.sharding import PartitionSpec as P

MESH = pl.DeviceIdType.MESH
F32 = jnp.float32
BF16 = jnp.bfloat16
VMEM = pl.BlockSpec(memory_space=pltpu.VMEM)
HBM = pl.BlockSpec(memory_space=pl.ANY)


def coords():
    s, k = lax.axis_index("space"), lax.axis_index("vec")
    return s // 4, (s // 2) % 2, s % 2, k // 4, k % 4


def lane_of(shape):
    return lax.broadcasted_iota(jnp.int32, shape, len(shape) - 1)


STEPS = ((2, 2), (1, 2), (3, 2), (2, 1), (2, 3), (1, 1), (3, 3), (1, 3),
         (3, 1), (2, 0), (0, 2), (0, 1), (0, 3), (1, 0), (3, 0), (0, 0))


def halves(t):
    hi = t.astype(BF16)
    return hi, (t - hi.astype(F32)).astype(BF16)


def apply_link(link, field):
    out = []
    for i in range(3):
        re = im = None
        for j in range(3):
            ur, ui = link(i, j)
            fr, fi = field[j]
            a = ur * fr - ui * fi
            b = ur * fi + ui * fr
            re = a if re is None else re + a
            im = b if im is None else im + b
        out.append((re, im))
    return out


def kernel(mom_ref, dir_ref, x_ref, u_ref, out_ref,
           stage, lstage, v_ref, up_ref, dn_ref, lk_ref, ulo_ref,
           left, right02, right1, tab, e_ref, cin, cs, yin, ys, xin, xs, zst, zin, zs, lin,
           send, recv, lsend, lrecv, fsend, frecv, usend, urecv,
           csend, crecv, asend, arecv, bsend, brecv, zsend, zrecv, tsend, trecv):
    y, xh, c, xl, z = coords()
    s, k = lax.axis_index("space"), lax.axis_index("vec")
    x = xh * 2 + xl
    selfish = c == xh

    def dev(y_, x_, c_, z_):
        return (y_ * 2 + x_ // 2) * 2 + c_, (x_ % 2) * 4 + z_

    def on_y(d):
        return dev((y + d) % 4, x, c, z)

    def on_x(d):
        return dev(y, (x + d) % 4, c, z)

    def on_z(d):
        return dev(y, x, c, (z + d) % 4)

    partner = dev(y, x, 1 - c, z)
    twin = dev(y, xh * 2 + 1 - xl, c, z)
    q = 2 * y + c
    qn, qp = (q + 1) % 8, (q + 7) % 8
    s_next = (qn // 2 * 2 + xh) * 2 + qn % 2
    s_prev = (qp // 2 * 2 + xh) * 2 + qp % 2

    def target(i):
        xt, zt = (x + STEPS[i][0]) % 4, (z + STEPS[i][1]) % 4
        return (y * 2 + xt // 2) * 2 + xh, (xt % 2) * 4 + zt, xt * 4 + zt

    def origin(i):
        return (y * 2 + c) * 2 + i % 2, i // 2

    barrier = pltpu.get_barrier_semaphore()

    def greet(i):
        st, kt, _j = target(i)

        @pl.when(jnp.logical_or(st != s, kt != k))
        def _():
            pl.semaphore_signal(barrier, inc=1, device_id=(st, kt), device_id_type=MESH)

        so, ko = origin(i)

        @pl.when(jnp.logical_or(so != s, ko != k))
        def _():
            pl.semaphore_signal(barrier, inc=1, device_id=(so, ko), device_id_type=MESH)

    for i in range(16):
        greet(i)
    pl.semaphore_signal(barrier, inc=1, device_id=(s_next, k), device_id_type=MESH)
    pl.semaphore_signal(barrier, inc=1, device_id=(s_prev, k), device_id_type=MESH)

    pl.semaphore_signal(barrier, inc=1, device_id=partner, device_id_type=MESH)
    for d in (1, 2, 3):
        for on in (on_y, on_x, on_z):
            pl.semaphore_signal(barrier, inc=1, device_id=on(d), device_id_type=MESH)

    for xt in range(2):
        j = (xt * 2 + xl) * 4 + z
        lstage[xt, 48:56, :] = jnp.zeros((8, 128), F32)
        lstage[xt, 0:54, :] = u_ref[pl.ds(j, 54, stride=16), :]
    pl.semaphore_wait(barrier, jnp.where(selfish, 42, 44))

    def link_copy(xt):
        return pltpu.make_async_remote_copy(
            src_ref=lstage.at[xt], dst_ref=lk_ref.at[c], send_sem=lsend.at[xt],
            recv_sem=lrecv.at[c], device_id=((y * 2 + xt) * 2 + xh, k), device_id_type=MESH)

    for xt in range(2):
        mine = jnp.logical_and(selfish, xh == xt)

        @pl.when(mine)
        def _():
            pltpu.make_async_copy(lstage.at[xt], lk_ref.at[c], lrecv.at[c]).start()

        @pl.when(jnp.logical_not(mine))
        def _():
            link_copy(xt).start()

    lane = lane_of((144, 128))

    def main_copy(i):
        st, kt, j = target(i)
        return pltpu.make_async_remote_copy(
            src_ref=stage.at[i], dst_ref=v_ref.at[c, k], send_sem=send.at[i],
            recv_sem=recv.at[c * 8 + k], device_id=(st, kt), device_id_type=MESH)

    def put(i):
        st, kt, j = target(i)
        nxt = (j + 1) % 16
        stage[i, 0:288, :] = x_ref[pl.ds(j, 288, stride=16), :]
        re = x_ref[pl.ds(nxt, 144, stride=16), :]
        im = x_ref[pl.ds(144 * 16 + nxt, 144, stride=16), :]
        stage[i, 288:432, :] = jnp.where(lane < 64, re, pltpu.roll(im, 64, 1))
        mine = jnp.logical_and(st == s, kt == k)

        @pl.when(mine)
        def _():
            pltpu.make_async_copy(stage.at[i], v_ref.at[c, k], recv.at[c * 8 + k]).start()

        @pl.when(jnp.logical_not(mine))
        def _():
            main_copy(i).start()

    for i in range(16):
        put(i)

    for p in range(2):
        pltpu.make_async_copy(lk_ref.at[p], lk_ref.at[p], lrecv.at[p]).wait()
    ulo = pltpu.make_async_remote_copy(
        src_ref=lk_ref.at[1, pl.ds(0, 24)], dst_ref=ulo_ref, send_sem=usend,
        recv_sem=urecv, device_id=(s_next, k), device_id_type=MESH)
    ulo.start()

    def hand(p, vb):
        return pltpu.make_async_remote_copy(
            src_ref=v_ref.at[p, vb, pl.ds(0, 288)],
            dst_ref=(up_ref if p == 0 else dn_ref).at[vb],
            send_sem=fsend.at[p, vb], recv_sem=frecv.at[p, vb],
            device_id=(s_prev if p == 0 else s_next, k), device_id_type=MESH)

    line = (xh * 2 + xl) * 4 + z
    lane1 = lane_of((8, 128))
    low1 = lane1 < 64
    for mm in range(2):
        for place in range(3):
            plane = 4 * y + 2 * c + (jnp.where(low1, 0, 1) if place == 2 else place)
            row = 2 * line + (2 if place == 2 else jnp.where(low1, 0, 1))
            col = lane1 & 63
            n = (((mom_ref[mm, 0] * plane) & 15) * 4 + ((mom_ref[mm, 1] * row) & 31) * 2
                 + ((mom_ref[mm, 2] * col) & 63)) & 63
            theta = n.astype(F32) * (2.0 * jnp.pi / 64)
            tab[mm, place, 0] = jnp.cos(theta)
            tab[mm, place, 1] = jnp.sin(theta)

    rows = 16
    lane = lane_of((rows, 128))
    low = lane < 64
    col = lane & 63

    def tools(vb, sub):
        at = pl.multiple_of(vb * 48 + sub * rows, rows)

        def comp(ref, reim, col_, *lead):
            first = pl.multiple_of(reim * 144 + col_ * 48 + sub * rows, rows)
            return ref[(*lead, vb, pl.ds(first, rows), slice(None))]

        def link(ref, mu_, dagger, *lead):
            def get(i, j):
                a, b = (j, i) if dagger else (i, j)
                r = mu_ * 18 + a * 3 + b
                ur = ref[(*lead, pl.ds(r, 1), slice(None))]
                ui = ref[(*lead, pl.ds(r + 9, 1), slice(None))]
                return ur, (-ui if dagger else ui)
            return get

        def put_right(mu_, place, cc, dr, di):
            kk = pl.ds((6 + cc if place == 2 else cc * 2 + place) * 128, 128)
            to = right1 if mu_ == 1 else right02
            off = pl.ds(pl.multiple_of(at + (384 if mu_ == 2 else 0), rows), rows)
            for i, t in enumerate((dr, di - dr, dr + di)):
                hi, lo = halves(t)
                to[i, 0, off, kk] = hi
                to[i, 1, off, kk] = lo

        return at, comp, link, put_right

    def inside(vb, sub):
        at, comp, link, put_right = tools(vb, sub)
        v = [[(comp(v_ref, 0, cc, p), comp(v_ref, 1, cc, p)) for cc in range(3)] for p in range(2)]
        packed = []
        for p in range(2):
            packed.append([
                v_ref[p, vb, pl.ds(pl.multiple_of(288 + cc * 48 + sub * rows, rows), rows), :]
                for cc in range(3)])
        ext = [
            (jnp.where(low, packed[0][cc], pltpu.roll(packed[1][cc], 64, 1)),
             jnp.where(low, pltpu.roll(packed[0][cc], 64, 1), packed[1][cc]))
            for cc in range(3)]

        for mm in range(2):
            for place in range(3):
                co, si = tab[mm, place, 0, 0:1], tab[mm, place, 1, 0:1]
                for cc in range(3):
                    vr, vi = ext[cc] if place == 2 else v[place][cc]
                    lr = vr * co - vi * si
                    li = -(vr * si + vi * co)
                    kk = pl.ds((6 + cc if place == 2 else cc * 2 + place) * 128, 128)
                    for i, t in enumerate((lr + li, lr, li)):
                        hi, lo = halves(t)
                        left[mm, i, 0, pl.ds(at, rows), kk] = hi
                        left[mm, i, 1, pl.ds(at, rows), kk] = lo

        spill = []
        for p in range(2):
            shifted = []
            for cc in range(3):
                vr, vi = v[p][cc]
                shifted.append((
                    pltpu.roll(jnp.where(low, packed[p][cc], vr), 64, 1),
                    jnp.where(low, pltpu.roll(vi, 64, 1), packed[p][cc])))
            fwd = apply_link(link(lk_ref, 1, False, p), shifted)
            bwd = apply_link(link(lk_ref, 1, True, p), v[p])
            turned = []
            for cc in range(3):
                tr, ti = pltpu.roll(bwd[cc][0], 64, 1), pltpu.roll(bwd[cc][1], 64, 1)
                turned.append((tr, ti))
                put_right(1, p, cc, fwd[cc][0] - jnp.where(low, 0.0, tr),
                          fwd[cc][1] - jnp.where(low, 0.0, ti))
            spill.append((bwd, turned))
            def ahead(t):
                return jnp.where(col == 63, pltpu.roll(t, 63, 1), pltpu.roll(t, 127, 1))

            def behind(t):
                return jnp.where(col == 0, pltpu.roll(t, 65, 1), pltpu.roll(t, 1, 1))

            fwd = apply_link(link(lk_ref, 2, False, p), [(ahead(a), ahead(b)) for a, b in v[p]])
            bwd = apply_link(link(lk_ref, 2, True, p), v[p])
            for cc in range(3):
                put_right(2, p, cc, fwd[cc][0] - behind(bwd[cc][0]),
                          fwd[cc][1] - behind(bwd[cc][1]))
        for cc in range(3):
            put_right(1, 2, cc,
                      -jnp.where(low, spill[0][1][cc][0], spill[1][0][cc][0]),
                      -jnp.where(low, spill[0][1][cc][1], spill[1][0][cc][1]))

    def across(vb, sub):
        at, comp, link, put_right = tools(vb, sub)
        v = [[(comp(v_ref, 0, cc, p), comp(v_ref, 1, cc, p)) for cc in range(3)] for p in range(2)]
        above = [(comp(up_ref, 0, cc), comp(up_ref, 1, cc)) for cc in range(3)]
        below = [(comp(dn_ref, 0, cc), comp(dn_ref, 1, cc)) for cc in range(3)]
        for p in range(2):
            fwd = apply_link(link(lk_ref, 0, False, p), v[1] if p == 0 else above)
            bwd = (apply_link(link(ulo_ref, 0, True), below) if p == 0
                   else apply_link(link(lk_ref, 0, True, 0), v[0]))
            for cc in range(3):
                put_right(0, p, cc, fwd[cc][0] - bwd[cc][0], fwd[cc][1] - bwd[cc][1])

    def arrivals(other):
        number = 0
        for far in range(2):
            for low_ in range(2):
                digits = [
                    xs_ * 4 + dz for dx, dz in STEPS for xs_ in range(2)
                    if (2 * far + low_ - xs_) % 4 == dx]
                value = sum(t * 8 ** n for n, t in enumerate(digits))
                hit = jnp.logical_and((xh != c) == ((far == 1) != other), xl == low_)
                number = jnp.where(hit, value, number)
        return number

    def vector_block(number):
        digit = number % 8
        return digit // 4 * 4 + (z + 4 - digit % 4) % 4

    def take(t, number):
        vb = vector_block(number)
        for p in range(2):
            pltpu.make_async_copy(v_ref.at[p, vb], v_ref.at[p, vb], recv.at[p * 8 + vb]).wait()
            hand(p, vb).start()

        def sub_loop(sub, _):
            inside(vb, sub)
            return 0

        lax.fori_loop(0, 3, sub_loop, 0)
        return number // 8

    lax.fori_loop(0, 8, take, arrivals(False))
    ulo.wait_recv()

    def join(t, number):
        vb = vector_block(number)
        for p in range(2):
            hand(p, vb).wait_recv()

        def sub_loop(sub, _):
            across(vb, sub)
            return 0

        lax.fori_loop(0, 3, sub_loop, 0)
        return number // 8

    lax.fori_loop(0, 8, join, arrivals(True))

    dims = (((1,), (1,)), ((), ()))
    dot = functools.partial(lax.dot_general, dimension_numbers=dims, preferred_element_type=F32)

    def product_pair(m):
        def one(i):
            d = pl.ds(0, 768)
            lh, ll = left[m, i, 0, :, d], left[m, i, 1, :, d]
            rh, rl = right02[i, 0], right02[i, 1]
            return dot(lh, rh) + dot(lh, rl) + dot(ll, rh)

        def keep(ri, t):
            e_ref[3 * m, ri] = t[:, 0:384].reshape(8, 2, 24, 384)
            e_ref[3 * m + 1, ri] = t[:, 384:768].reshape(8, 2, 24, 384)

        k1 = one(0)
        keep(0, k1 - one(2))
        keep(1, k1 + one(1))

    def product_one(m):
        def one(i):
            lh, ll = left[m, i, 0], left[m, i, 1]
            rh, rl = right1[i, 0], right1[i, 1]
            return (dot(lh, rh) + dot(lh, rl) + dot(ll, rh)).reshape(8, 2, 24, 384)

        k1 = one(0)
        e_ref[3 * m + 2, 0] = k1 - one(2)
        e_ref[3 * m + 2, 1] = k1 + one(1)

    def core_copy(b):
        return pltpu.make_async_remote_copy(
            src_ref=e_ref.at[b, :, :, 1 - c], dst_ref=cin.at[b], send_sem=csend.at[b],
            recv_sem=crecv.at[b], device_id=partner, device_id_type=MESH)

    def first(b, d, even):
        if even:
            src, to = cs.at[b, :, (y + d) % 4], on_y(d)
            dst = yin.at[b // 2, d - 1]
        else:
            xt = (x + d) % 4
            src, to = cs.at[b, xt % 2, :, xt // 2], on_x(d)
            dst = xin.at[b // 2, d - 1]
        return pltpu.make_async_remote_copy(
            src_ref=src, dst_ref=dst, send_sem=asend.at[b, d - 1],
            recv_sem=arecv.at[b, d - 1], device_id=to, device_id_type=MESH)

    def second(b, d, even):
        if even:
            xt = (x + d) % 4
            src, to = ys.at[b // 2, xt % 2, xt // 2], on_x(d)
        else:
            src, to = xs.at[b // 2, (y + d) % 4], on_y(d)
        return pltpu.make_async_remote_copy(
            src_ref=src, dst_ref=lin.at[b, d - 1], send_sem=bsend.at[b, d - 1],
            recv_sem=brecv.at[b, d - 1], device_id=to, device_id_type=MESH)

    def third(d):
        return pltpu.make_async_remote_copy(
            src_ref=zst.at[d], dst_ref=zin.at[d - 1], send_sem=zsend.at[d - 1],
            recv_sem=zrecv.at[d - 1], device_id=on_z(d), device_id_type=MESH)

    last = pltpu.make_async_remote_copy(
        src_ref=zs.at[0], dst_ref=zs.at[1], send_sem=tsend, recv_sem=trecv,
        device_id=twin, device_id_type=MESH)

    def by_order(b, act):
        if isinstance(b, int):
            act(b % 2 == 0)
            return

        @pl.when(b % 2 == 0)
        def _():
            act(True)

        @pl.when(b % 2 == 1)
        def _():
            act(False)

    def over_core(b):
        core_copy(b).wait_recv()
        for i in range(8):
            for ri in range(2):
                cs[b, ri, i // 2, i % 2] = e_ref[b, ri, i, c] + cin[b, ri, i]

        def go(even):
            for d in (1, 2, 3):
                first(b, d, even).start()

        by_order(b, go)

    def over_first(b):
        h = b // 2

        def go(even):
            for d in (1, 2, 3):
                first(b, d, even).wait_recv()
            if even:
                for ri in range(2):
                    for g in range(2):
                        ys[h, ri, g] = (cs[b, ri, y, g] + yin[h, 0, ri, g]) + (
                            yin[h, 1, ri, g] + yin[h, 2, ri, g])
            else:
                for i in range(4):
                    xs[h, i] = (cs[b, xl, i, xh] + xin[h, 0, i]) + (xin[h, 1, i] + xin[h, 2, i])
            for d in (1, 2, 3):
                second(b, d, even).start()

        by_order(b, go)

    def over_second(b):
        def go(even):
            for d in (1, 2, 3):
                second(b, d, even).wait_recv()
            own = ys[b // 2, xl, xh] if even else xs[b // 2, y]
            t = (own + lin[b, 0]) + (lin[b, 1] + lin[b, 2])
            for d in range(4):
                zt = (z + d) % 4
                zst[d, b] = jnp.where(
                    lane_of((24, 128)) < 48,
                    pltpu.roll(t, (384 - 48 * zt) % 384, 1)[:, 0:128],
                    pltpu.roll(t, (624 - 48 * zt) % 384, 1)[:, 0:128])

        by_order(b, go)

    def turn(m, _):
        product_pair(m)
        core_copy(3 * m).start()
        core_copy(3 * m + 1).start()

        @pl.when(m == 1)
        def _():
            over_core(2)
            over_first(0)

        product_one(m)
        core_copy(3 * m + 2).start()
        over_core(3 * m)
        over_core(3 * m + 1)
        return 0

    lax.fori_loop(0, 2, turn, 0)
    over_core(5)
    over_first(1)
    over_first(2)
    over_second(0)
    over_second(1)
    over_first(3)
    over_second(2)
    over_first(4)
    over_second(3)
    over_first(5)
    over_second(4)
    over_second(5)

    for d in (1, 2, 3):
        third(d).start()
    for d in (1, 2, 3):
        third(d).wait_recv()
    zs[0] = (zst[0] + zin[0]) + (zin[1] + zin[2])
    last.start()
    last.wait_recv()
    def mine(which, b):
        return pltpu.roll(zs[which, b], (128 - 48 * xl) % 128, 1)[:, 0:48]

    for m in range(2):
        for which in range(2):
            d0, d2, d1 = (mine(which, 3 * m + i) for i in range(3))
            for n in range(3):
                d = dir_ref[n]
                out_ref[m, n, xl if which == 0 else 1 - xl] = jnp.where(
                    d == 0, d0, jnp.where(d == 1, d1, d2))
    last.wait_send()
    for d in (1, 2, 3):
        third(d).wait_send()

    def gone(b, _):
        core_copy(b).wait_send()

        def go(even):
            for d in (1, 2, 3):
                first(b, d, even).wait_send()
                second(b, d, even).wait_send()

        by_order(b, go)
        return 0

    lax.fori_loop(0, 6, gone, 0)

    def finish(i, _):
        for p in range(2):
            hand(p, i).wait_send()
        return 0

    lax.fori_loop(0, 8, finish, 0)
    ulo.wait_send()
    for xt in range(2):

        @pl.when(jnp.logical_not(jnp.logical_and(selfish, xh == xt)))
        def _():
            link_copy(xt).wait_send()

    def sent(i):
        st, kt, _j = target(i)

        @pl.when(jnp.logical_or(st != s, kt != k))
        def _():
            main_copy(i).wait_send()

    for i in range(16):
        sent(i)


def elementals(vectors, links, momenta, directions):
    dma = pltpu.SemaphoreType.DMA
    smem = pl.BlockSpec(memory_space=pltpu.SMEM)
    return pl.pallas_call(
        kernel,
        out_shape=jax.ShapeDtypeStruct((2, 3, 2, 24, 48), F32),
        in_specs=[smem, smem, VMEM, VMEM],
        out_specs=VMEM,
        scratch_shapes=[
            pltpu.VMEM((16, 432, 128), F32),
            pltpu.VMEM((2, 56, 128), F32),
            pltpu.VMEM((2, 8, 432, 128), F32),
            pltpu.VMEM((8, 288, 128), F32),
            pltpu.VMEM((8, 288, 128), F32),
            pltpu.VMEM((2, 56, 128), F32),
            pltpu.VMEM((24, 128), F32),
            pltpu.VMEM((2, 3, 2, 384, 1152), BF16),
            pltpu.VMEM((3, 2, 768, 768), BF16),
            pltpu.VMEM((3, 2, 384, 1152), BF16),
            pltpu.VMEM((2, 3, 2, 8, 128), F32),
            pltpu.VMEM((6, 2, 8, 2, 24, 384), F32),
            pltpu.VMEM((6, 2, 8, 24, 384), F32),
            pltpu.VMEM((6, 2, 4, 2, 24, 384), F32),
            pltpu.VMEM((3, 3, 2, 2, 24, 384), F32),
            pltpu.VMEM((3, 2, 2, 24, 384), F32),
            pltpu.VMEM((3, 3, 4, 24, 384), F32),
            pltpu.VMEM((3, 4, 24, 384), F32),
            pltpu.VMEM((4, 6, 24, 128), F32),
            pltpu.VMEM((3, 6, 24, 128), F32),
            pltpu.VMEM((2, 6, 24, 128), F32),
            pltpu.VMEM((6, 3, 24, 384), F32),
            dma((16,)), dma((16,)), dma((2,)), dma((2,)),
            dma((2, 8)), dma((2, 8)), dma(()), dma(()),
            dma((6,)), dma((6,)), dma((6, 3)), dma((6, 3)), dma((6, 3)), dma((6, 3)),
            dma((3,)), dma((3,)), dma(()), dma(()),
        ],
        compiler_params=pltpu.CompilerParams(
            collective_id=0, has_side_effects=True, vmem_limit_bytes=60 << 20),
        cost_estimate=pl.CostEstimate(flops=2 * 18 * 3 * 384 * 384 * 896, bytes_accessed=6 << 20, transcendentals=0),
        name="elementals",
    )(momenta, directions, vectors.reshape(288 * 16, 128), links.reshape(54 * 16, 128))


def solution(mesh):
    placed = (
        P(None, None, "vec", "space", None),
        P(None, None, None, None, "space", None),
        P(),
        P(),
    )
    return jax.shard_map(
        elementals,
        mesh=mesh,
        in_specs=placed,
        out_specs=P(None, None, None, "space", "vec"),
        check_vma=False,
    )
```

```python
import functools

import jax
import jax.numpy as jnp
from jax import lax
from jax.experimental import pallas as pl
from jax.experimental.pallas import tpu as pltpu
from jax.sharding import PartitionSpec as P

MESH = pl.DeviceIdType.MESH
F32 = jnp.float32
BF16 = jnp.bfloat16
VMEM = pl.BlockSpec(memory_space=pltpu.VMEM)
HBM = pl.BlockSpec(memory_space=pl.ANY)


def coords():
    s, k = lax.axis_index("space"), lax.axis_index("vec")
    return s // 4, (s // 2) % 2, s % 2, k // 4, k % 4


def lane_of(shape):
    return lax.broadcasted_iota(jnp.int32, shape, len(shape) - 1)


STEPS = ((2, 2), (1, 2), (3, 2), (2, 1), (2, 3), (1, 1), (3, 3), (1, 3),
         (3, 1), (2, 0), (0, 2), (0, 1), (0, 3), (1, 0), (3, 0), (0, 0))


def halves(t):
    hi = t.astype(BF16)
    return hi, (t - hi.astype(F32)).astype(BF16)


def apply_link(link, field):
    out = []
    for i in range(3):
        re = im = None
        for j in range(3):
            ur, ui = link(i, j)
            fr, fi = field[j]
            a = ur * fr - ui * fi
            b = ur * fi + ui * fr
            re = a if re is None else re + a
            im = b if im is None else im + b
        out.append((re, im))
    return out


def kernel(mom_ref, dir_ref, x_ref, u_ref, out_ref,
           stage, lstage, v_ref, up_ref, dn_ref, lk_ref, ulo_ref,
           left, right02, right1, tab, e_ref, cin, cs, yin, ys, xin, xs, zst, zin, lin,
           send, recv, lsend, lrecv, fsend, frecv, usend, urecv,
           csend, crecv, asend, arecv, bsend, brecv, zsend, zrecv):
    y, xh, c, xl, z = coords()
    s, k = lax.axis_index("space"), lax.axis_index("vec")
    x = xh * 2 + xl
    selfish = c == xh

    def dev(y_, x_, c_, z_):
        return (y_ * 2 + x_ // 2) * 2 + c_, (x_ % 2) * 4 + z_

    def on_y(d):
        return dev((y + d) % 4, x, c, z)

    def on_x(d):
        return dev(y, (x + d) % 4, c, z)

    def on_z(d):
        return dev(y, x, c, (z + d) % 4)

    partner = dev(y, x, 1 - c, z)
    s_turned = (z * 2 + xh) * 2 + c
    q = 2 * y + c
    qn, qp = (q + 1) % 8, (q + 7) % 8
    s_next = (qn // 2 * 2 + xh) * 2 + qn % 2
    s_prev = (qp // 2 * 2 + xh) * 2 + qp % 2

    def target(i):
        xt, zt = (x + STEPS[i][0]) % 4, (z + STEPS[i][1]) % 4
        return (y * 2 + xt // 2) * 2 + xh, (xt % 2) * 4 + zt, xt * 4 + zt

    def origin(i):
        return (y * 2 + c) * 2 + i % 2, i // 2

    barrier = pltpu.get_barrier_semaphore()

    def greet(i):
        st, kt, _j = target(i)

        @pl.when(jnp.logical_or(st != s, kt != k))
        def _():
            pl.semaphore_signal(barrier, inc=1, device_id=(st, kt), device_id_type=MESH)

        so, ko = origin(i)

        @pl.when(jnp.logical_or(so != s, ko != k))
        def _():
            pl.semaphore_signal(barrier, inc=1, device_id=(so, ko), device_id_type=MESH)

    for i in range(16):
        greet(i)
    pl.semaphore_signal(barrier, inc=1, device_id=(s_next, k), device_id_type=MESH)
    pl.semaphore_signal(barrier, inc=1, device_id=(s_prev, k), device_id_type=MESH)

    pl.semaphore_signal(barrier, inc=1, device_id=partner, device_id_type=MESH)
    for d in (1, 2, 3):
        for on in (on_y, on_x):
            pl.semaphore_signal(barrier, inc=1, device_id=on(d), device_id_type=MESH)
    for kt in range(8):

        @pl.when(kt != k)
        def _():
            pl.semaphore_signal(barrier, inc=1, device_id=(s, kt), device_id_type=MESH)

        @pl.when(jnp.logical_or(s_turned != s, kt != k))
        def _():
            pl.semaphore_signal(barrier, inc=1, device_id=(s_turned, kt), device_id_type=MESH)

        so, ko = (kt % 4 * 2 + xh) * 2 + c, kt // 4 * 4 + y

        @pl.when(jnp.logical_or(so != s, ko != k))
        def _():
            pl.semaphore_signal(barrier, inc=1, device_id=(so, ko), device_id_type=MESH)

    for xt in range(2):
        j = (xt * 2 + xl) * 4 + z
        lstage[xt, 48:56, :] = jnp.zeros((8, 128), F32)
        lstage[xt, 0:54, :] = u_ref[pl.ds(j, 54, stride=16), :]
    pl.semaphore_wait(barrier, jnp.where(selfish, 62, 64) - jnp.where(y == z, 2, 0))

    def link_copy(xt):
        return pltpu.make_async_remote_copy(
            src_ref=lstage.at[xt], dst_ref=lk_ref.at[c], send_sem=lsend.at[xt],
            recv_sem=lrecv.at[c], device_id=((y * 2 + xt) * 2 + xh, k), device_id_type=MESH)

    for xt in range(2):
        mine = jnp.logical_and(selfish, xh == xt)

        @pl.when(mine)
        def _():
            pltpu.make_async_copy(lstage.at[xt], lk_ref.at[c], lrecv.at[c]).start()

        @pl.when(jnp.logical_not(mine))
        def _():
            link_copy(xt).start()

    lane = lane_of((144, 128))

    def main_copy(i):
        st, kt, j = target(i)
        return pltpu.make_async_remote_copy(
            src_ref=stage.at[i], dst_ref=v_ref.at[c, k], send_sem=send.at[i],
            recv_sem=recv.at[c * 8 + k], device_id=(st, kt), device_id_type=MESH)

    def put(i):
        st, kt, j = target(i)
        nxt = (j + 1) % 16
        stage[i, 0:288, :] = x_ref[pl.ds(j, 288, stride=16), :]
        re = x_ref[pl.ds(nxt, 144, stride=16), :]
        im = x_ref[pl.ds(144 * 16 + nxt, 144, stride=16), :]
        stage[i, 288:432, :] = jnp.where(lane < 64, re, pltpu.roll(im, 64, 1))
        mine = jnp.logical_and(st == s, kt == k)

        @pl.when(mine)
        def _():
            pltpu.make_async_copy(stage.at[i], v_ref.at[c, k], recv.at[c * 8 + k]).start()

        @pl.when(jnp.logical_not(mine))
        def _():
            main_copy(i).start()

    for i in range(16):
        put(i)

    for p in range(2):
        pltpu.make_async_copy(lk_ref.at[p], lk_ref.at[p], lrecv.at[p]).wait()
    ulo = pltpu.make_async_remote_copy(
        src_ref=lk_ref.at[1, pl.ds(0, 24)], dst_ref=ulo_ref, send_sem=usend,
        recv_sem=urecv, device_id=(s_next, k), device_id_type=MESH)
    ulo.start()

    def hand(p, vb):
        return pltpu.make_async_remote_copy(
            src_ref=v_ref.at[p, vb, pl.ds(0, 288)],
            dst_ref=(up_ref if p == 0 else dn_ref).at[vb],
            send_sem=fsend.at[p, vb], recv_sem=frecv.at[p, vb],
            device_id=(s_prev if p == 0 else s_next, k), device_id_type=MESH)

    line = (xh * 2 + xl) * 4 + z
    lane1 = lane_of((8, 128))
    low1 = lane1 < 64
    for mm in range(2):
        for place in range(3):
            plane = 4 * y + 2 * c + (jnp.where(low1, 0, 1) if place == 2 else place)
            row = 2 * line + (2 if place == 2 else jnp.where(low1, 0, 1))
            col = lane1 & 63
            n = (((mom_ref[mm, 0] * plane) & 15) * 4 + ((mom_ref[mm, 1] * row) & 31) * 2
                 + ((mom_ref[mm, 2] * col) & 63)) & 63
            theta = n.astype(F32) * (2.0 * jnp.pi / 64)
            tab[mm, place, 0] = jnp.cos(theta)
            tab[mm, place, 1] = jnp.sin(theta)

    rows = 16
    lane = lane_of((rows, 128))
    low = lane < 64
    col = lane & 63

    def tools(vb, sub):
        at = pl.multiple_of(vb * 48 + sub * rows, rows)

        def comp(ref, reim, col_, *lead):
            first = pl.multiple_of(reim * 144 + col_ * 48 + sub * rows, rows)
            return ref[(*lead, vb, pl.ds(first, rows), slice(None))]

        def link(ref, mu_, dagger, *lead):
            def get(i, j):
                a, b = (j, i) if dagger else (i, j)
                r = mu_ * 18 + a * 3 + b
                ur = ref[(*lead, pl.ds(r, 1), slice(None))]
                ui = ref[(*lead, pl.ds(r + 9, 1), slice(None))]
                return ur, (-ui if dagger else ui)
            return get

        def put_right(mu_, place, cc, dr, di):
            kk = pl.ds((6 + cc if place == 2 else cc * 2 + place) * 128, 128)
            to = right1 if mu_ == 1 else right02
            off = pl.ds(pl.multiple_of(at + (384 if mu_ == 2 else 0), rows), rows)
            for i, t in enumerate((dr, di - dr, dr + di)):
                hi, lo = halves(t)
                to[i, 0, off, kk] = hi
                to[i, 1, off, kk] = lo

        return at, comp, link, put_right

    def inside(vb, sub):
        at, comp, link, put_right = tools(vb, sub)
        v = [[(comp(v_ref, 0, cc, p), comp(v_ref, 1, cc, p)) for cc in range(3)] for p in range(2)]
        packed = []
        for p in range(2):
            packed.append([
                v_ref[p, vb, pl.ds(pl.multiple_of(288 + cc * 48 + sub * rows, rows), rows), :]
                for cc in range(3)])
        ext = [
            (jnp.where(low, packed[0][cc], pltpu.roll(packed[1][cc], 64, 1)),
             jnp.where(low, pltpu.roll(packed[0][cc], 64, 1), packed[1][cc]))
            for cc in range(3)]

        for mm in range(2):
            for place in range(3):
                co, si = tab[mm, place, 0, 0:1], tab[mm, place, 1, 0:1]
                for cc in range(3):
                    vr, vi = ext[cc] if place == 2 else v[place][cc]
                    lr = vr * co - vi * si
                    li = -(vr * si + vi * co)
                    kk = pl.ds((6 + cc if place == 2 else cc * 2 + place) * 128, 128)
                    for i, t in enumerate((lr + li, lr, li)):
                        hi, lo = halves(t)
                        left[mm, i, 0, pl.ds(at, rows), kk] = hi
                        left[mm, i, 1, pl.ds(at, rows), kk] = lo

        spill = []
        for p in range(2):
            shifted = []
            for cc in range(3):
                vr, vi = v[p][cc]
                shifted.append((
                    pltpu.roll(jnp.where(low, packed[p][cc], vr), 64, 1),
                    jnp.where(low, pltpu.roll(vi, 64, 1), packed[p][cc])))
            fwd = apply_link(link(lk_ref, 1, False, p), shifted)
            bwd = apply_link(link(lk_ref, 1, True, p), v[p])
            turned = []
            for cc in range(3):
                tr, ti = pltpu.roll(bwd[cc][0], 64, 1), pltpu.roll(bwd[cc][1], 64, 1)
                turned.append((tr, ti))
                put_right(1, p, cc, fwd[cc][0] - jnp.where(low, 0.0, tr),
                          fwd[cc][1] - jnp.where(low, 0.0, ti))
            spill.append((bwd, turned))
            def ahead(t):
                return jnp.where(col == 63, pltpu.roll(t, 63, 1), pltpu.roll(t, 127, 1))

            def behind(t):
                return jnp.where(col == 0, pltpu.roll(t, 65, 1), pltpu.roll(t, 1, 1))

            fwd = apply_link(link(lk_ref, 2, False, p), [(ahead(a), ahead(b)) for a, b in v[p]])
            bwd = apply_link(link(lk_ref, 2, True, p), v[p])
            for cc in range(3):
                put_right(2, p, cc, fwd[cc][0] - behind(bwd[cc][0]),
                          fwd[cc][1] - behind(bwd[cc][1]))
        for cc in range(3):
            put_right(1, 2, cc,
                      -jnp.where(low, spill[0][1][cc][0], spill[1][0][cc][0]),
                      -jnp.where(low, spill[0][1][cc][1], spill[1][0][cc][1]))

    def across(vb, sub):
        at, comp, link, put_right = tools(vb, sub)
        v = [[(comp(v_ref, 0, cc, p), comp(v_ref, 1, cc, p)) for cc in range(3)] for p in range(2)]
        above = [(comp(up_ref, 0, cc), comp(up_ref, 1, cc)) for cc in range(3)]
        below = [(comp(dn_ref, 0, cc), comp(dn_ref, 1, cc)) for cc in range(3)]
        for p in range(2):
            fwd = apply_link(link(lk_ref, 0, False, p), v[1] if p == 0 else above)
            bwd = (apply_link(link(ulo_ref, 0, True), below) if p == 0
                   else apply_link(link(lk_ref, 0, True, 0), v[0]))
            for cc in range(3):
                put_right(0, p, cc, fwd[cc][0] - bwd[cc][0], fwd[cc][1] - bwd[cc][1])

    def arrivals(other):
        number = 0
        for far in range(2):
            for low_ in range(2):
                digits = [
                    xs_ * 4 + dz for dx, dz in STEPS for xs_ in range(2)
                    if (2 * far + low_ - xs_) % 4 == dx]
                value = sum(t * 8 ** n for n, t in enumerate(digits))
                hit = jnp.logical_and((xh != c) == ((far == 1) != other), xl == low_)
                number = jnp.where(hit, value, number)
        return number

    def vector_block(number):
        digit = number % 8
        return digit // 4 * 4 + (z + 4 - digit % 4) % 4

    def take(t, number):
        vb = vector_block(number)
        for p in range(2):
            pltpu.make_async_copy(v_ref.at[p, vb], v_ref.at[p, vb], recv.at[p * 8 + vb]).wait()
            hand(p, vb).start()

        def sub_loop(sub, _):
            inside(vb, sub)
            return 0

        lax.fori_loop(0, 3, sub_loop, 0)
        return number // 8

    lax.fori_loop(0, 8, take, arrivals(False))

    def join(t, number):
        vb = vector_block(number)
        for p in range(2):
            hand(p, vb).wait_recv()

        def sub_loop(sub, _):
            across(vb, sub)
            return 0

        lax.fori_loop(0, 3, sub_loop, 0)
        return number // 8

    dims = (((1,), (1,)), ((), ()))
    dot = functools.partial(lax.dot_general, dimension_numbers=dims, preferred_element_type=F32)

    def one(m, i):
        lh, ll = left[m, i, 0], left[m, i, 1]
        rh, rl = right1[i, 0], right1[i, 1]
        return (dot(lh, rh) + dot(lh, rl) + dot(ll, rh)).reshape(8, 2, 24, 384)

    def one_real(m):
        k1 = one(m, 0)
        e_ref[m, 1] = k1
        e_ref[m, 0] = k1 - one(m, 2)
        core_copy(m, 0).start()

    def one_imag(m):
        e_ref[m, 1] += one(m, 1)
        core_copy(m, 1).start()

    def pair(m, i):
        d = pl.ds(0, 768)
        lh, ll = left[m, i, 0, :, d], left[m, i, 1, :, d]
        rh, rl = right02[i, 0], right02[i, 1]
        t = dot(lh, rh) + dot(lh, rl) + dot(ll, rh)
        return t[:, 0:384].reshape(8, 2, 24, 384), t[:, 384:768].reshape(8, 2, 24, 384)

    def pair_real(m):
        b = 2 + 2 * m
        for n, t in enumerate(pair(m, 0)):
            e_ref[b + n, 1] = t
        for n, t in enumerate(pair(m, 2)):
            e_ref[b + n, 0] = e_ref[b + n, 1] - t
            core_copy(b + n, 0).start()

    def pair_imag(m):
        b = 2 + 2 * m
        for n, t in enumerate(pair(m, 1)):
            e_ref[b + n, 1] += t
            core_copy(b + n, 1).start()

    def core_copy(b, ri):
        return pltpu.make_async_remote_copy(
            src_ref=e_ref.at[b, ri, :, 1 - c], dst_ref=cin.at[b, ri], send_sem=csend.at[b, ri],
            recv_sem=crecv.at[b, ri], device_id=partner, device_id_type=MESH)

    slot = {0: 0, 1: 1, 2: 2, 4: 3, 3: 0, 5: 1}

    def rows_first(b, d, ri):
        at, to = (z, on_z) if b < 2 else (y, on_y)
        return pltpu.make_async_remote_copy(
            src_ref=cs.at[b, ri, (at + d) % 4], dst_ref=yin.at[slot[b], d - 1, ri],
            send_sem=asend.at[b, 3 * ri + d - 1], recv_sem=arecv.at[b, 3 * ri + d - 1],
            device_id=to(d), device_id_type=MESH)

    def x_first(b, d):
        xt = (x + d) % 4
        return pltpu.make_async_remote_copy(
            src_ref=cs.at[b, xt % 2, :, xt // 2], dst_ref=xin.at[slot[b], d - 1],
            send_sem=asend.at[b, d - 1], recv_sem=arecv.at[b, d - 1],
            device_id=on_x(d), device_id_type=MESH)

    def by_rows(b):
        return b not in (3, 5)

    def second(b, d):
        if by_rows(b):
            xt = (x + d) % 4
            src, to = ys.at[slot[b], xt % 2, xt // 2], on_x(d)
        else:
            src, to = xs.at[slot[b], (y + d) % 4], on_y(d)
        return pltpu.make_async_remote_copy(
            src_ref=src, dst_ref=lin.at[b, d - 1], send_sem=bsend.at[b, d - 1],
            recv_sem=brecv.at[b, d - 1], device_id=to, device_id_type=MESH)

    def third(n, kt):
        at = xl * 4 + y if n == 0 else k
        return pltpu.make_async_remote_copy(
            src_ref=zst.at[n, kt], dst_ref=zin.at[n, at], send_sem=zsend.at[n, kt],
            recv_sem=zrecv.at[n, at], device_id=(s_turned if n == 0 else s, kt), device_id_type=MESH)

    def away(n, kt):
        return jnp.logical_or(y != z, kt != k) if n == 0 else kt != k

    def over_core(b, ri):
        core_copy(b, ri).wait_recv()
        for i in range(8):
            cs[b, ri, i // 2, i % 2] = e_ref[b, ri, i, c] + cin[b, ri, i]
        for d in (1, 2, 3):
            if by_rows(b):
                rows_first(b, d, ri).start()
            else:

                @pl.when((x + d) % 2 == ri)
                def _():
                    x_first(b, d).start()

    def over_first(b):
        n = slot[b]
        if by_rows(b):
            q = z if b < 2 else y
            for ri in range(2):
                for d in (1, 2, 3):
                    rows_first(b, d, ri).wait_recv()
                for g in range(2):
                    ys[n, ri, g] = (cs[b, ri, q, g] + yin[n, 0, ri, g]) + (
                        yin[n, 1, ri, g] + yin[n, 2, ri, g])
        else:
            for d in (1, 2, 3):
                x_first(b, d).wait_recv()
            for i in range(4):
                xs[n, i] = (cs[b, xl, i, xh] + xin[n, 0, i]) + (xin[n, 1, i] + xin[n, 2, i])
        for d in (1, 2, 3):
            second(b, d).start()

    def over_second(n):
        sums = []
        for b in (2 * n, 2 * n + 1):
            for d in (1, 2, 3):
                second(b, d).wait_recv()
            own = ys[slot[b], xl, xh] if by_rows(b) else xs[slot[b], y]
            sums.append((own + lin[b, 0]) + (lin[b, 1] + lin[b, 2]))
        first_half = lane_of((24, 128)) < 64
        for kt in range(8):
            zst[n, kt] = jnp.where(
                first_half,
                pltpu.roll(sums[0], (384 - 48 * kt) % 384, 1)[:, 0:128],
                pltpu.roll(sums[1], (448 - 48 * kt) % 384, 1)[:, 0:128])

            @pl.when(away(n, kt))
            def _():
                third(n, kt).start()

        if n == 0:

            @pl.when(y == z)
            def _():
                zin[n, k] = zst[n, k]
        else:
            zin[n, k] = zst[n, k]

    one_real(0)
    one_imag(0)
    over_core(0, 0)
    ulo.wait_recv()
    lax.fori_loop(0, 8, join, arrivals(True))
    over_core(0, 1)
    pair_real(0)
    pair_imag(0)
    over_core(2, 0)
    over_core(3, 0)
    pair_real(1)
    over_core(2, 1)
    over_core(3, 1)
    over_first(0)
    pair_imag(1)
    over_core(4, 0)
    over_core(5, 0)
    one_real(1)
    over_core(4, 1)
    over_core(5, 1)
    one_imag(1)
    over_core(1, 0)
    over_first(2)
    over_first(3)
    over_core(1, 1)
    over_first(4)
    over_first(5)
    over_second(1)
    over_first(1)
    over_second(2)
    over_second(0)

    def arrive(n):
        for kt in range(8):

            @pl.when(away(n, kt))
            def _():
                pltpu.make_async_copy(zin.at[n, kt], zin.at[n, kt], zrecv.at[n, kt]).wait()

    for n in range(3):
        arrive(n)
    done = {}
    for n in range(3):
        for ri in range(2):
            t = (zin[n, 4 * ri] + zin[n, 4 * ri + 1]) + (zin[n, 4 * ri + 2] + zin[n, 4 * ri + 3])
            done[2 * n, ri] = t[:, 0:48]
            done[2 * n + 1, ri] = pltpu.roll(t, 64, 1)[:, 0:48]
    for m in range(2):
        for ri in range(2):
            d0, d1, d2 = done[2 + 2 * m, ri], done[m, ri], done[3 + 2 * m, ri]
            for n in range(3):
                d = dir_ref[n]
                out_ref[m, n, ri] = jnp.where(d == 0, d0, jnp.where(d == 1, d1, d2))
    for n in range(3):
        for kt in range(8):

            @pl.when(away(n, kt))
            def _():
                third(n, kt).wait_send()
    for b in range(6):
        for ri in range(2):
            core_copy(b, ri).wait_send()
        for d in (1, 2, 3):
            second(b, d).wait_send()
            if by_rows(b):
                rows_first(b, d, 0).wait_send()
                rows_first(b, d, 1).wait_send()
            else:
                x_first(b, d).wait_send()

    def finish(i, _):
        for p in range(2):
            hand(p, i).wait_send()
        return 0

    lax.fori_loop(0, 8, finish, 0)
    ulo.wait_send()
    for xt in range(2):

        @pl.when(jnp.logical_not(jnp.logical_and(selfish, xh == xt)))
        def _():
            link_copy(xt).wait_send()

    def sent(i):
        st, kt, _j = target(i)

        @pl.when(jnp.logical_or(st != s, kt != k))
        def _():
            main_copy(i).wait_send()

    for i in range(16):
        sent(i)


def elementals(vectors, links, momenta, directions):
    dma = pltpu.SemaphoreType.DMA
    smem = pl.BlockSpec(memory_space=pltpu.SMEM)
    return pl.pallas_call(
        kernel,
        out_shape=jax.ShapeDtypeStruct((2, 3, 2, 24, 48), F32),
        in_specs=[smem, smem, VMEM, VMEM],
        out_specs=VMEM,
        scratch_shapes=[
            pltpu.VMEM((16, 432, 128), F32),
            pltpu.VMEM((2, 56, 128), F32),
            pltpu.VMEM((2, 8, 432, 128), F32),
            pltpu.VMEM((8, 288, 128), F32),
            pltpu.VMEM((8, 288, 128), F32),
            pltpu.VMEM((2, 56, 128), F32),
            pltpu.VMEM((24, 128), F32),
            pltpu.VMEM((2, 3, 2, 384, 1152), BF16),
            pltpu.VMEM((3, 2, 768, 768), BF16),
            pltpu.VMEM((3, 2, 384, 1152), BF16),
            pltpu.VMEM((2, 3, 2, 8, 128), F32),
            pltpu.VMEM((6, 2, 8, 2, 24, 384), F32),
            pltpu.VMEM((6, 2, 8, 24, 384), F32),
            pltpu.VMEM((6, 2, 4, 2, 24, 384), F32),
            pltpu.VMEM((4, 3, 2, 2, 24, 384), F32),
            pltpu.VMEM((4, 2, 2, 24, 384), F32),
            pltpu.VMEM((2, 3, 4, 24, 384), F32),
            pltpu.VMEM((2, 4, 24, 384), F32),
            pltpu.VMEM((3, 8, 24, 128), F32),
            pltpu.VMEM((3, 8, 24, 128), F32),
            pltpu.VMEM((6, 3, 24, 384), F32),
            dma((16,)), dma((16,)), dma((2,)), dma((2,)),
            dma((2, 8)), dma((2, 8)), dma(()), dma(()),
            dma((6, 2)), dma((6, 2)), dma((6, 6)), dma((6, 6)), dma((6, 3)), dma((6, 3)),
            dma((3, 8)), dma((3, 8)),
        ],
        compiler_params=pltpu.CompilerParams(
            collective_id=0, has_side_effects=True, vmem_limit_bytes=60 << 20),
        cost_estimate=pl.CostEstimate(flops=2 * 18 * 3 * 384 * 384 * 896, bytes_accessed=6 << 20, transcendentals=0),
        name="elementals",
    )(momenta, directions, vectors.reshape(288 * 16, 128), links.reshape(54 * 16, 128))


def solution(mesh):
    placed = (
        P(None, None, "vec", "space", None),
        P(None, None, None, None, "space", None),
        P(),
        P(),
    )
    return jax.shard_map(
        elementals,
        mesh=mesh,
        in_specs=placed,
        out_specs=P(None, None, None, "space", "vec"),
        check_vma=False,
    )
```

```python
import functools

import jax
import jax.numpy as jnp
from jax import lax
from jax.experimental import pallas as pl
from jax.experimental.pallas import tpu as pltpu
from jax.sharding import PartitionSpec as P

MESH = pl.DeviceIdType.MESH
F32 = jnp.float32
BF16 = jnp.bfloat16
VMEM = pl.BlockSpec(memory_space=pltpu.VMEM)
HBM = pl.BlockSpec(memory_space=pl.ANY)


def coords():
    s, k = lax.axis_index("space"), lax.axis_index("vec")
    return s // 4, (s // 2) % 2, s % 2, k // 4, k % 4


def lane_of(shape):
    return lax.broadcasted_iota(jnp.int32, shape, len(shape) - 1)


STEPS = ((2, 2), (1, 2), (3, 2), (2, 1), (2, 3), (1, 1), (3, 3), (1, 3),
         (3, 1), (2, 0), (0, 2), (0, 1), (0, 3), (1, 0), (3, 0), (0, 0))


def halves(t):
    hi = t.astype(BF16)
    return hi, (t - hi.astype(F32)).astype(BF16)


def apply_link(link, field):
    out = []
    for i in range(3):
        re = im = None
        for j in range(3):
            ur, ui = link(i, j)
            fr, fi = field[j]
            a = ur * fr - ui * fi
            b = ur * fi + ui * fr
            re = a if re is None else re + a
            im = b if im is None else im + b
        out.append((re, im))
    return out


def kernel(mom_ref, dir_ref, x_hbm, u_ref, out_ref,
           x_ref, xsem, stage, lstage, v_ref, up_ref, dn_ref, lk_ref, ulo_ref,
           left, right02, right1, tab, e_ref, cin, cs, yin, ys, xin, xs, zst, zin, lin,
           send, recv, lsend, lrecv, fsend, frecv, usend, urecv,
           csend, crecv, asend, arecv, bsend, brecv, zsend, zrecv):
    y, xh, c, xl, z = coords()
    s, k = lax.axis_index("space"), lax.axis_index("vec")
    x = xh * 2 + xl
    selfish = c == xh

    def dev(y_, x_, c_, z_):
        return (y_ * 2 + x_ // 2) * 2 + c_, (x_ % 2) * 4 + z_

    def on_y(d):
        return dev((y + d) % 4, x, c, z)

    def on_x(d):
        return dev(y, (x + d) % 4, c, z)

    def on_z(d):
        return dev(y, x, c, (z + d) % 4)

    partner = dev(y, x, 1 - c, z)
    s_turned = (z * 2 + xh) * 2 + c
    q = 2 * y + c
    qn, qp = (q + 1) % 8, (q + 7) % 8
    s_next = (qn // 2 * 2 + xh) * 2 + qn % 2
    s_prev = (qp // 2 * 2 + xh) * 2 + qp % 2

    def target(i, step=None):
        dx, dz = STEPS[i] if step is None else step
        xt, zt = (x + dx) % 4, (z + dz) % 4
        return (y * 2 + xt // 2) * 2 + xh, (xt % 2) * 4 + zt, xt * 4 + zt

    def origin(i):
        return (y * 2 + c) * 2 + i % 2, i // 2

    fetch = pltpu.make_async_copy(x_hbm, x_ref, xsem)
    fetch.start()
    barrier = pltpu.get_barrier_semaphore()

    def greet(i):
        st, kt, _j = target(i)

        @pl.when(jnp.logical_or(st != s, kt != k))
        def _():
            pl.semaphore_signal(barrier, inc=1, device_id=(st, kt), device_id_type=MESH)

        so, ko = origin(i)

        @pl.when(jnp.logical_or(so != s, ko != k))
        def _():
            pl.semaphore_signal(barrier, inc=1, device_id=(so, ko), device_id_type=MESH)

    for i in range(16):
        greet(i)
    pl.semaphore_signal(barrier, inc=1, device_id=(s_next, k), device_id_type=MESH)
    pl.semaphore_signal(barrier, inc=1, device_id=(s_prev, k), device_id_type=MESH)

    pl.semaphore_signal(barrier, inc=1, device_id=partner, device_id_type=MESH)
    for d in (1, 2, 3):
        for on in (on_y, on_x):
            pl.semaphore_signal(barrier, inc=1, device_id=on(d), device_id_type=MESH)
    for kt in range(8):

        @pl.when(kt != k)
        def _():
            pl.semaphore_signal(barrier, inc=1, device_id=(s, kt), device_id_type=MESH)

        @pl.when(jnp.logical_or(s_turned != s, kt != k))
        def _():
            pl.semaphore_signal(barrier, inc=1, device_id=(s_turned, kt), device_id_type=MESH)

        so, ko = (kt % 4 * 2 + xh) * 2 + c, kt // 4 * 4 + y

        @pl.when(jnp.logical_or(so != s, ko != k))
        def _():
            pl.semaphore_signal(barrier, inc=1, device_id=(so, ko), device_id_type=MESH)

    for xt in range(2):
        j = (xt * 2 + xl) * 4 + z
        lstage[xt, 48:56, :] = jnp.zeros((8, 128), F32)
        lstage[xt, 0:54, :] = u_ref[pl.ds(j, 54, stride=16), :]
    pl.semaphore_wait(barrier, jnp.where(selfish, 62, 64) - jnp.where(y == z, 2, 0))

    def link_copy(xt):
        return pltpu.make_async_remote_copy(
            src_ref=lstage.at[xt], dst_ref=lk_ref.at[c], send_sem=lsend.at[xt],
            recv_sem=lrecv.at[c], device_id=((y * 2 + xt) * 2 + xh, k), device_id_type=MESH)

    for xt in range(2):
        mine = jnp.logical_and(selfish, xh == xt)

        @pl.when(mine)
        def _():
            pltpu.make_async_copy(lstage.at[xt], lk_ref.at[c], lrecv.at[c]).start()

        @pl.when(jnp.logical_not(mine))
        def _():
            link_copy(xt).start()


    def main_copy(i, part, step=None):
        st, kt, j = target(i, step)
        r = pl.ds(part * 144, 144)
        return pltpu.make_async_remote_copy(
            src_ref=stage.at[i, r], dst_ref=v_ref.at[c, k, r], send_sem=send.at[part, i],
            recv_sem=recv.at[part, c * 8 + k], device_id=(st, kt), device_id_type=MESH)

    def arrived(p, vb, part):
        r = pl.ds(part * 144, 144)
        pltpu.make_async_copy(
            v_ref.at[p, vb, r], v_ref.at[p, vb, r], recv.at[part, p * 8 + vb]).wait()

    def put(i, part, step=None):
        st, kt, j = target(i, step)
        r = pl.ds(part * 144, 144)
        if part < 2:
            stage[i, r, :] = x_ref[pl.ds(part * 144 * 16 + j, 144, stride=16), :]
        else:
            nxt = (j + 1) % 16
            re = x_ref[pl.ds(nxt, 144, stride=16), :]
            im = x_ref[pl.ds(144 * 16 + nxt, 144, stride=16), :]
            stage[i, r, :] = jnp.where(lane_of((144, 128)) < 64, re, pltpu.roll(im, 64, 1))
        mine = jnp.logical_and(st == s, kt == k)

        @pl.when(mine)
        def _():
            pltpu.make_async_copy(
                stage.at[i, r], v_ref.at[c, k, r], recv.at[part, c * 8 + k]).start()

        @pl.when(jnp.logical_not(mine))
        def _():
            main_copy(i, part, step).start()

    fetch.wait()
    for i in range(16):
        put(i, 0)

    packed_steps = tuple(
        sum(STEPS[2 * n + odd][axis] * 4 ** n for n in range(8))
        for odd in range(2) for axis in range(2))

    def put_two(t, part, steps):
        for odd in range(2):
            put(2 * t + odd, part, (steps[2 * odd] % 4, steps[2 * odd + 1] % 4))
        return tuple(n // 4 for n in steps)

    for p in range(2):
        pltpu.make_async_copy(lk_ref.at[p], lk_ref.at[p], lrecv.at[p]).wait()
    ulo = pltpu.make_async_remote_copy(
        src_ref=lk_ref.at[1, pl.ds(0, 24)], dst_ref=ulo_ref, send_sem=usend,
        recv_sem=urecv, device_id=(s_next, k), device_id_type=MESH)
    ulo.start()

    def hand(p, vb, part):
        r = pl.ds(part * 144, 144)
        return pltpu.make_async_remote_copy(
            src_ref=v_ref.at[p, vb, r],
            dst_ref=(up_ref if p == 0 else dn_ref).at[vb, r],
            send_sem=fsend.at[part, p, vb], recv_sem=frecv.at[part, p, vb],
            device_id=(s_prev if p == 0 else s_next, k), device_id_type=MESH)

    line = (xh * 2 + xl) * 4 + z
    lane1 = lane_of((8, 128))
    low1 = lane1 < 64
    for mm in range(2):
        for place in range(3):
            plane = 4 * y + 2 * c + (jnp.where(low1, 0, 1) if place == 2 else place)
            row = 2 * line + (2 if place == 2 else jnp.where(low1, 0, 1))
            col = lane1 & 63
            n = (((mom_ref[mm, 0] * plane) & 15) * 4 + ((mom_ref[mm, 1] * row) & 31) * 2
                 + ((mom_ref[mm, 2] * col) & 63)) & 63
            theta = n.astype(F32) * (2.0 * jnp.pi / 64)
            tab[mm, place, 0] = jnp.cos(theta)
            tab[mm, place, 1] = jnp.sin(theta)

    rows = 16
    lane = lane_of((rows, 128))
    low = lane < 64
    col = lane & 63

    def tools(vb, sub):
        at = pl.multiple_of(vb * 48 + sub * rows, rows)

        def comp(ref, reim, col_, *lead):
            first = pl.multiple_of(reim * 144 + col_ * 48 + sub * rows, rows)
            return ref[(*lead, vb, pl.ds(first, rows), slice(None))]

        def link(ref, mu_, dagger, *lead):
            def get(i, j):
                a, b = (j, i) if dagger else (i, j)
                r = mu_ * 18 + a * 3 + b
                ur = ref[(*lead, pl.ds(r, 1), slice(None))]
                ui = ref[(*lead, pl.ds(r + 9, 1), slice(None))]
                return ur, (-ui if dagger else ui)
            return get

        def put_right(mu_, place, cc, dr, di):
            kk = pl.ds((6 + cc if place == 2 else cc * 2 + place) * 128, 128)
            to = right1 if mu_ == 1 else right02
            off = pl.ds(pl.multiple_of(at + (384 if mu_ == 2 else 0), rows), rows)
            for i, t in enumerate((dr, di - dr, dr + di)):
                hi, lo = halves(t)
                to[i, 0, off, kk] = hi
                to[i, 1, off, kk] = lo

        return at, comp, link, put_right

    def vectors_of(comp):
        return [[(comp(v_ref, 0, cc, p), comp(v_ref, 1, cc, p)) for cc in range(3)] for p in range(2)]

    def put_left(at, place, field):
        for mm in range(2):
            co, si = tab[mm, place, 0, 0:1], tab[mm, place, 1, 0:1]
            for cc in range(3):
                vr, vi = field[cc]
                lr = vr * co - vi * si
                li = -(vr * si + vi * co)
                kk = pl.ds((6 + cc if place == 2 else cc * 2 + place) * 128, 128)
                for i, t in enumerate((lr + li, lr, li)):
                    hi, lo = halves(t)
                    left[mm, i, 0, pl.ds(at, rows), kk] = hi
                    left[mm, i, 1, pl.ds(at, rows), kk] = lo

    def inside(vb, sub):
        at, comp, link, put_right = tools(vb, sub)
        v = vectors_of(comp)

        def ahead(t):
            return jnp.where(col == 63, pltpu.roll(t, 63, 1), pltpu.roll(t, 127, 1))

        def behind(t):
            return jnp.where(col == 0, pltpu.roll(t, 65, 1), pltpu.roll(t, 1, 1))

        for p in range(2):
            put_left(at, p, v[p])
            fwd = apply_link(link(lk_ref, 2, False, p), [(ahead(a), ahead(b)) for a, b in v[p]])
            bwd = apply_link(link(lk_ref, 2, True, p), v[p])
            for cc in range(3):
                put_right(2, p, cc, fwd[cc][0] - behind(bwd[cc][0]),
                          fwd[cc][1] - behind(bwd[cc][1]))

    def along(vb, sub):
        at, comp, link, put_right = tools(vb, sub)
        v = vectors_of(comp)
        packed = []
        for p in range(2):
            packed.append([
                v_ref[p, vb, pl.ds(pl.multiple_of(288 + cc * 48 + sub * rows, rows), rows), :]
                for cc in range(3)])
        put_left(at, 2, [
            (jnp.where(low, packed[0][cc], pltpu.roll(packed[1][cc], 64, 1)),
             jnp.where(low, pltpu.roll(packed[0][cc], 64, 1), packed[1][cc]))
            for cc in range(3)])
        spill = []
        for p in range(2):
            shifted = []
            for cc in range(3):
                vr, vi = v[p][cc]
                shifted.append((
                    pltpu.roll(jnp.where(low, packed[p][cc], vr), 64, 1),
                    jnp.where(low, pltpu.roll(vi, 64, 1), packed[p][cc])))
            fwd = apply_link(link(lk_ref, 1, False, p), shifted)
            bwd = apply_link(link(lk_ref, 1, True, p), v[p])
            turned = []
            for cc in range(3):
                tr, ti = pltpu.roll(bwd[cc][0], 64, 1), pltpu.roll(bwd[cc][1], 64, 1)
                turned.append((tr, ti))
                put_right(1, p, cc, fwd[cc][0] - jnp.where(low, 0.0, tr),
                          fwd[cc][1] - jnp.where(low, 0.0, ti))
            spill.append((bwd, turned))
        for cc in range(3):
            put_right(1, 2, cc,
                      -jnp.where(low, spill[0][1][cc][0], spill[1][0][cc][0]),
                      -jnp.where(low, spill[0][1][cc][1], spill[1][0][cc][1]))

    def across(vb, sub):
        at, comp, link, put_right = tools(vb, sub)
        v = [[(comp(v_ref, 0, cc, p), comp(v_ref, 1, cc, p)) for cc in range(3)] for p in range(2)]
        above = [(comp(up_ref, 0, cc), comp(up_ref, 1, cc)) for cc in range(3)]
        below = [(comp(dn_ref, 0, cc), comp(dn_ref, 1, cc)) for cc in range(3)]
        for p in range(2):
            fwd = apply_link(link(lk_ref, 0, False, p), v[1] if p == 0 else above)
            bwd = (apply_link(link(ulo_ref, 0, True), below) if p == 0
                   else apply_link(link(lk_ref, 0, True, 0), v[0]))
            for cc in range(3):
                put_right(0, p, cc, fwd[cc][0] - bwd[cc][0], fwd[cc][1] - bwd[cc][1])

    def arrivals(other):
        number = 0
        for far in range(2):
            for low_ in range(2):
                digits = [
                    xs_ * 4 + dz for dx, dz in STEPS for xs_ in range(2)
                    if (2 * far + low_ - xs_) % 4 == dx]
                value = sum(t * 8 ** n for n, t in enumerate(digits))
                hit = jnp.logical_and((xh != c) == ((far == 1) != other), xl == low_)
                number = jnp.where(hit, value, number)
        return number

    def vector_block(number):
        digit = number % 8
        return digit // 4 * 4 + (z + 4 - digit % 4) % 4

    def take_real(t, carry):
        number, steps = carry
        steps = put_two(t, 1, steps)
        vb = vector_block(number)
        for p in range(2):
            arrived(p, vb, 0)
            hand(p, vb, 0).start()
        return number // 8, steps

    def take(t, carry):
        number, steps = carry
        steps = put_two(t, 2, steps)
        vb = vector_block(number)
        for p in range(2):
            arrived(p, vb, 1)
            hand(p, vb, 1).start()

        def sub_loop(sub, _):
            inside(vb, sub)
            return 0

        lax.fori_loop(0, 3, sub_loop, 0)
        return number // 8, steps

    begin = arrivals(False), tuple(jnp.int32(n) for n in packed_steps)
    lax.fori_loop(0, 8, take_real, begin)
    lax.fori_loop(0, 8, take, begin)

    def join(t, number):
        vb = vector_block(number)
        for p in range(2):
            hand(p, vb, 0).wait_recv()
            hand(p, vb, 1).wait_recv()

        def sub_loop(sub, _):
            across(vb, sub)
            return 0

        lax.fori_loop(0, 3, sub_loop, 0)
        return number // 8

    def late(t, number):
        vb = vector_block(number)
        for p in range(2):
            arrived(p, vb, 2)

        def sub_loop(sub, _):
            along(vb, sub)
            return 0

        lax.fori_loop(0, 3, sub_loop, 0)
        return number // 8

    dims = (((1,), (1,)), ((), ()))
    dot = functools.partial(lax.dot_general, dimension_numbers=dims, preferred_element_type=F32)

    def one(m, i):
        lh, ll = left[m, i, 0], left[m, i, 1]
        rh, rl = right1[i, 0], right1[i, 1]
        return (dot(lh, rh) + dot(lh, rl) + dot(ll, rh)).reshape(8, 2, 24, 384)

    def one_real(m):
        k1 = one(m, 0)
        e_ref[m, 1] = k1
        e_ref[m, 0] = k1 - one(m, 2)
        core_copy(m, 0).start()

    def one_imag(m):
        e_ref[m, 1] += one(m, 1)
        core_copy(m, 1).start()

    def pair(m, i):
        d = pl.ds(0, 768)
        lh, ll = left[m, i, 0, :, d], left[m, i, 1, :, d]
        rh, rl = right02[i, 0], right02[i, 1]
        t = dot(lh, rh) + dot(lh, rl) + dot(ll, rh)
        return t[:, 0:384].reshape(8, 2, 24, 384), t[:, 384:768].reshape(8, 2, 24, 384)

    def pair_real(m):
        b = 2 + 2 * m
        for n, t in enumerate(pair(m, 0)):
            e_ref[b + n, 1] = t
        for n, t in enumerate(pair(m, 2)):
            e_ref[b + n, 0] = e_ref[b + n, 1] - t
            core_copy(b + n, 0).start()

    def pair_imag(m):
        b = 2 + 2 * m
        for n, t in enumerate(pair(m, 1)):
            e_ref[b + n, 1] += t
            core_copy(b + n, 1).start()

    def core_copy(b, ri):
        return pltpu.make_async_remote_copy(
            src_ref=e_ref.at[b, ri, :, 1 - c], dst_ref=cin.at[b, ri], send_sem=csend.at[b, ri],
            recv_sem=crecv.at[b, ri], device_id=partner, device_id_type=MESH)

    slot = {2: 0, 3: 1, 0: 2, 4: 3, 1: 0, 5: 1}

    def rows_first(b, d, ri):
        at, to = (z, on_z) if b in (2, 3) else (y, on_y)
        return pltpu.make_async_remote_copy(
            src_ref=cs.at[b, ri, (at + d) % 4], dst_ref=yin.at[slot[b], d - 1, ri],
            send_sem=asend.at[b, 3 * ri + d - 1], recv_sem=arecv.at[b, 3 * ri + d - 1],
            device_id=to(d), device_id_type=MESH)

    def x_first(b, d):
        xt = (x + d) % 4
        return pltpu.make_async_remote_copy(
            src_ref=cs.at[b, xt % 2, :, xt // 2], dst_ref=xin.at[slot[b], d - 1],
            send_sem=asend.at[b, d - 1], recv_sem=arecv.at[b, d - 1],
            device_id=on_x(d), device_id_type=MESH)

    def by_rows(b):
        return b not in (1, 5)

    def second(b, d):
        if by_rows(b):
            xt = (x + d) % 4
            src, to = ys.at[slot[b], xt % 2, xt // 2], on_x(d)
        else:
            src, to = xs.at[slot[b], (y + d) % 4], on_y(d)
        return pltpu.make_async_remote_copy(
            src_ref=src, dst_ref=lin.at[b, d - 1], send_sem=bsend.at[b, d - 1],
            recv_sem=brecv.at[b, d - 1], device_id=to, device_id_type=MESH)

    def third(n, kt):
        at = xl * 4 + y if n == 1 else k
        return pltpu.make_async_remote_copy(
            src_ref=zst.at[n, kt], dst_ref=zin.at[n, at], send_sem=zsend.at[n, kt],
            recv_sem=zrecv.at[n, at], device_id=(s_turned if n == 1 else s, kt), device_id_type=MESH)

    def away(n, kt):
        return jnp.logical_or(y != z, kt != k) if n == 1 else kt != k

    def over_core(b, ri):
        core_copy(b, ri).wait_recv()
        for i in range(8):
            cs[b, ri, i // 2, i % 2] = e_ref[b, ri, i, c] + cin[b, ri, i]
        for d in (1, 2, 3):
            if by_rows(b):
                rows_first(b, d, ri).start()
            else:

                @pl.when((x + d) % 2 == ri)
                def _():
                    x_first(b, d).start()

    def over_first(b):
        n = slot[b]
        if by_rows(b):
            q = z if b in (2, 3) else y
            for ri in range(2):
                for d in (1, 2, 3):
                    rows_first(b, d, ri).wait_recv()
                for g in range(2):
                    ys[n, ri, g] = (cs[b, ri, q, g] + yin[n, 0, ri, g]) + (
                        yin[n, 1, ri, g] + yin[n, 2, ri, g])
        else:
            for d in (1, 2, 3):
                x_first(b, d).wait_recv()
            for i in range(4):
                xs[n, i] = (cs[b, xl, i, xh] + xin[n, 0, i]) + (xin[n, 1, i] + xin[n, 2, i])
        for d in (1, 2, 3):
            second(b, d).start()

    def over_second(n):
        sums = []
        for b in (2 * n, 2 * n + 1):
            for d in (1, 2, 3):
                second(b, d).wait_recv()
            own = ys[slot[b], xl, xh] if by_rows(b) else xs[slot[b], y]
            sums.append((own + lin[b, 0]) + (lin[b, 1] + lin[b, 2]))
        first_half = lane_of((24, 128)) < 64
        for kt in range(8):
            zst[n, kt] = jnp.where(
                first_half,
                pltpu.roll(sums[0], (384 - 48 * kt) % 384, 1)[:, 0:128],
                pltpu.roll(sums[1], (448 - 48 * kt) % 384, 1)[:, 0:128])

            @pl.when(away(n, kt))
            def _():
                third(n, kt).start()

        if n == 1:

            @pl.when(y == z)
            def _():
                zin[n, k] = zst[n, k]
        else:
            zin[n, k] = zst[n, k]

    ulo.wait_recv()
    lax.fori_loop(0, 8, join, arrivals(True))
    pair_real(0)
    pair_imag(0)
    over_core(2, 0)
    over_core(3, 0)
    pair_real(1)
    over_core(2, 1)
    over_core(3, 1)
    pair_imag(1)
    over_core(4, 0)
    over_core(5, 0)
    lax.fori_loop(0, 8, late, arrivals(False))
    over_core(4, 1)
    over_core(5, 1)
    one_real(0)
    over_first(2)
    over_first(3)
    one_imag(0)
    over_core(0, 0)
    over_first(4)
    over_first(5)
    one_real(1)
    over_core(0, 1)
    over_second(1)
    one_imag(1)
    over_core(1, 0)
    over_second(2)
    over_core(1, 1)
    over_first(0)
    over_first(1)
    over_second(0)

    def arrive(n):
        for kt in range(8):

            @pl.when(away(n, kt))
            def _():
                pltpu.make_async_copy(zin.at[n, kt], zin.at[n, kt], zrecv.at[n, kt]).wait()

    for n in range(3):
        arrive(n)
    done = {}
    for n in range(3):
        for ri in range(2):
            t = (zin[n, 4 * ri] + zin[n, 4 * ri + 1]) + (zin[n, 4 * ri + 2] + zin[n, 4 * ri + 3])
            done[2 * n, ri] = t[:, 0:48]
            done[2 * n + 1, ri] = pltpu.roll(t, 64, 1)[:, 0:48]
    for m in range(2):
        for ri in range(2):
            d0, d1, d2 = done[2 + 2 * m, ri], done[m, ri], done[3 + 2 * m, ri]
            for n in range(3):
                d = dir_ref[n]
                out_ref[m, n, ri] = jnp.where(d == 0, d0, jnp.where(d == 1, d1, d2))
    for n in range(3):
        for kt in range(8):

            @pl.when(away(n, kt))
            def _():
                third(n, kt).wait_send()
    for b in range(6):
        for ri in range(2):
            core_copy(b, ri).wait_send()
        for d in (1, 2, 3):
            second(b, d).wait_send()
            if by_rows(b):
                rows_first(b, d, 0).wait_send()
                rows_first(b, d, 1).wait_send()
            else:
                x_first(b, d).wait_send()

    def finish(i, _):
        for p in range(2):
            hand(p, i, 0).wait_send()
            hand(p, i, 1).wait_send()
        return 0

    lax.fori_loop(0, 8, finish, 0)
    ulo.wait_send()
    for xt in range(2):

        @pl.when(jnp.logical_not(jnp.logical_and(selfish, xh == xt)))
        def _():
            link_copy(xt).wait_send()

    def sent(i):
        st, kt, _j = target(i)

        @pl.when(jnp.logical_or(st != s, kt != k))
        def _():
            for part in range(3):
                main_copy(i, part).wait_send()

    for i in range(16):
        sent(i)


def elementals(vectors, links, momenta, directions):
    dma = pltpu.SemaphoreType.DMA
    smem = pl.BlockSpec(memory_space=pltpu.SMEM)
    return pl.pallas_call(
        kernel,
        out_shape=jax.ShapeDtypeStruct((2, 3, 2, 24, 48), F32),
        in_specs=[smem, smem, HBM, VMEM],
        out_specs=VMEM,
        scratch_shapes=[
            pltpu.VMEM((288 * 16, 128), F32),
            dma(()),
            pltpu.VMEM((16, 432, 128), F32),
            pltpu.VMEM((2, 56, 128), F32),
            pltpu.VMEM((2, 8, 432, 128), F32),
            pltpu.VMEM((8, 288, 128), F32),
            pltpu.VMEM((8, 288, 128), F32),
            pltpu.VMEM((2, 56, 128), F32),
            pltpu.VMEM((24, 128), F32),
            pltpu.VMEM((2, 3, 2, 384, 1152), BF16),
            pltpu.VMEM((3, 2, 768, 768), BF16),
            pltpu.VMEM((3, 2, 384, 1152), BF16),
            pltpu.VMEM((2, 3, 2, 8, 128), F32),
            pltpu.VMEM((6, 2, 8, 2, 24, 384), F32),
            pltpu.VMEM((6, 2, 8, 24, 384), F32),
            pltpu.VMEM((6, 2, 4, 2, 24, 384), F32),
            pltpu.VMEM((4, 3, 2, 2, 24, 384), F32),
            pltpu.VMEM((4, 2, 2, 24, 384), F32),
            pltpu.VMEM((2, 3, 4, 24, 384), F32),
            pltpu.VMEM((2, 4, 24, 384), F32),
            pltpu.VMEM((3, 8, 24, 128), F32),
            pltpu.VMEM((3, 8, 24, 128), F32),
            pltpu.VMEM((6, 3, 24, 384), F32),
            dma((3, 16)), dma((3, 16)), dma((2,)), dma((2,)),
            dma((2, 2, 8)), dma((2, 2, 8)), dma(()), dma(()),
            dma((6, 2)), dma((6, 2)), dma((6, 6)), dma((6, 6)), dma((6, 3)), dma((6, 3)),
            dma((3, 8)), dma((3, 8)),
        ],
        compiler_params=pltpu.CompilerParams(
            collective_id=0, has_side_effects=True, vmem_limit_bytes=60 << 20),
        cost_estimate=pl.CostEstimate(flops=2 * 18 * 3 * 384 * 384 * 896, bytes_accessed=6 << 20, transcendentals=0),
        name="elementals",
    )(momenta, directions, vectors.reshape(288 * 16, 128), links.reshape(54 * 16, 128))


def solution(mesh):
    placed = (
        P(None, None, "vec", "space", None),
        P(None, None, None, None, "space", None),
        P(),
        P(),
    )
    return jax.shard_map(
        elementals,
        mesh=mesh,
        in_specs=placed,
        out_specs=P(None, None, None, "space", "vec"),
        check_vma=False,
    )
```

```python
import functools

import jax
import jax.numpy as jnp
from jax import lax
from jax.experimental import pallas as pl
from jax.experimental.pallas import tpu as pltpu
from jax.sharding import PartitionSpec as P

MESH = pl.DeviceIdType.MESH
F32 = jnp.float32
BF16 = jnp.bfloat16
VMEM = pl.BlockSpec(memory_space=pltpu.VMEM)
HBM = pl.BlockSpec(memory_space=pl.ANY)


def coords():
    s, k = lax.axis_index("space"), lax.axis_index("vec")
    return s // 4, (s // 2) % 2, s % 2, k // 4, k % 4


def lane_of(shape):
    return lax.broadcasted_iota(jnp.int32, shape, len(shape) - 1)


STEPS = ((1, 0), (0, 1), (3, 0), (0, 3), (2, 0), (0, 2), (1, 1), (3, 3),
         (1, 3), (3, 1), (1, 2), (2, 1), (3, 2), (2, 3), (2, 2), (0, 0))


def halves(t):
    hi = t.astype(BF16)
    return hi, (t - hi.astype(F32)).astype(BF16)


def apply_link(link, field):
    out = []
    for i in range(3):
        re = im = None
        for j in range(3):
            ur, ui = link(i, j)
            fr, fi = field[j]
            a = ur * fr - ui * fi
            b = ur * fi + ui * fr
            re = a if re is None else re + a
            im = b if im is None else im + b
        out.append((re, im))
    return out


def kernel(mom_ref, dir_ref, x_hbm, u_ref, out_ref,
           x_ref, xsem, stage, lstage, v_ref, up_ref, dn_ref, lk_ref, ulo_ref,
           left, right02, right1, tab, e_ref, cin, cs, yin, ys, xin, xs, zst, zin, lin,
           send, recv, lsend, lrecv, fsend, frecv, usend, urecv,
           csend, crecv, asend, arecv, bsend, brecv, zsend, zrecv):
    y, xh, c, xl, z = coords()
    s, k = lax.axis_index("space"), lax.axis_index("vec")
    x = xh * 2 + xl
    selfish = c == xh

    def dev(y_, x_, c_, z_):
        return (y_ * 2 + x_ // 2) * 2 + c_, (x_ % 2) * 4 + z_

    def on_y(d):
        return dev((y + d) % 4, x, c, z)

    def on_x(d):
        return dev(y, (x + d) % 4, c, z)

    def on_z(d):
        return dev(y, x, c, (z + d) % 4)

    partner = dev(y, x, 1 - c, z)
    s_turned = (z * 2 + xh) * 2 + c
    q = 2 * y + c
    qn, qp = (q + 1) % 8, (q + 7) % 8
    s_next = (qn // 2 * 2 + xh) * 2 + qn % 2
    s_prev = (qp // 2 * 2 + xh) * 2 + qp % 2

    def target(i, step=None):
        dx, dz = STEPS[i] if step is None else step
        xt, zt = (x + dx) % 4, (z + dz) % 4
        return (y * 2 + xt // 2) * 2 + xh, (xt % 2) * 4 + zt, xt * 4 + zt

    def origin(i):
        return (y * 2 + c) * 2 + i % 2, i // 2

    fetch = pltpu.make_async_copy(x_hbm, x_ref, xsem)
    fetch.start()
    barrier = pltpu.get_barrier_semaphore()

    def greet(i):
        st, kt, _j = target(i)

        @pl.when(jnp.logical_or(st != s, kt != k))
        def _():
            pl.semaphore_signal(barrier, inc=1, device_id=(st, kt), device_id_type=MESH)

        so, ko = origin(i)

        @pl.when(jnp.logical_or(so != s, ko != k))
        def _():
            pl.semaphore_signal(barrier, inc=1, device_id=(so, ko), device_id_type=MESH)

    for i in range(16):
        greet(i)
    pl.semaphore_signal(barrier, inc=1, device_id=(s_next, k), device_id_type=MESH)
    pl.semaphore_signal(barrier, inc=1, device_id=(s_prev, k), device_id_type=MESH)

    pl.semaphore_signal(barrier, inc=1, device_id=partner, device_id_type=MESH)
    for d in (1, 2, 3):
        for on in (on_y, on_x):
            pl.semaphore_signal(barrier, inc=1, device_id=on(d), device_id_type=MESH)
    for kt in range(8):

        @pl.when(kt != k)
        def _():
            pl.semaphore_signal(barrier, inc=1, device_id=(s, kt), device_id_type=MESH)

        @pl.when(jnp.logical_or(s_turned != s, kt != k))
        def _():
            pl.semaphore_signal(barrier, inc=1, device_id=(s_turned, kt), device_id_type=MESH)

        so, ko = (kt % 4 * 2 + xh) * 2 + c, kt // 4 * 4 + y

        @pl.when(jnp.logical_or(so != s, ko != k))
        def _():
            pl.semaphore_signal(barrier, inc=1, device_id=(so, ko), device_id_type=MESH)

    for xt in range(2):
        j = (xt * 2 + xl) * 4 + z
        lstage[xt, 48:56, :] = jnp.zeros((8, 128), F32)
        lstage[xt, 0:54, :] = u_ref[pl.ds(j, 54, stride=16), :]
    pl.semaphore_wait(barrier, jnp.where(selfish, 62, 64) - jnp.where(y == z, 2, 0))

    def link_copy(xt):
        return pltpu.make_async_remote_copy(
            src_ref=lstage.at[xt], dst_ref=lk_ref.at[c], send_sem=lsend.at[xt],
            recv_sem=lrecv.at[c], device_id=((y * 2 + xt) * 2 + xh, k), device_id_type=MESH)

    for xt in range(2):
        mine = jnp.logical_and(selfish, xh == xt)

        @pl.when(mine)
        def _():
            pltpu.make_async_copy(lstage.at[xt], lk_ref.at[c], lrecv.at[c]).start()

        @pl.when(jnp.logical_not(mine))
        def _():
            link_copy(xt).start()


    def main_copy(i, part, step=None):
        st, kt, j = target(i, step)
        r = pl.ds(part * 144, 144)
        return pltpu.make_async_remote_copy(
            src_ref=stage.at[i, r], dst_ref=v_ref.at[c, k, r], send_sem=send.at[part, i],
            recv_sem=recv.at[part, c * 8 + k], device_id=(st, kt), device_id_type=MESH)

    def arrived(p, vb, part):
        r = pl.ds(part * 144, 144)
        pltpu.make_async_copy(
            v_ref.at[p, vb, r], v_ref.at[p, vb, r], recv.at[part, p * 8 + vb]).wait()

    def put(i, part, step=None):
        st, kt, j = target(i, step)
        r = pl.ds(part * 144, 144)
        if part < 2:
            stage[i, r, :] = x_ref[pl.ds(part * 144 * 16 + j, 144, stride=16), :]
        else:
            nxt = (j + 1) % 16
            re = x_ref[pl.ds(nxt, 144, stride=16), :]
            im = x_ref[pl.ds(144 * 16 + nxt, 144, stride=16), :]
            stage[i, r, :] = jnp.where(lane_of((144, 128)) < 64, re, pltpu.roll(im, 64, 1))
        mine = jnp.logical_and(st == s, kt == k)

        @pl.when(mine)
        def _():
            pltpu.make_async_copy(
                stage.at[i, r], v_ref.at[c, k, r], recv.at[part, c * 8 + k]).start()

        @pl.when(jnp.logical_not(mine))
        def _():
            main_copy(i, part, step).start()

    fetch.wait()
    for i in range(16):
        put(i, 0)

    packed_steps = tuple(
        sum(STEPS[2 * n + odd][axis] * 4 ** n for n in range(8))
        for odd in range(2) for axis in range(2))

    def put_two(t, part, steps):
        for odd in range(2):
            put(2 * t + odd, part, (steps[2 * odd] % 4, steps[2 * odd + 1] % 4))
        return tuple(n // 4 for n in steps)

    for p in range(2):
        pltpu.make_async_copy(lk_ref.at[p], lk_ref.at[p], lrecv.at[p]).wait()
    ulo = pltpu.make_async_remote_copy(
        src_ref=lk_ref.at[1, pl.ds(0, 24)], dst_ref=ulo_ref, send_sem=usend,
        recv_sem=urecv, device_id=(s_next, k), device_id_type=MESH)
    ulo.start()

    def hand(p, vb, part):
        r = pl.ds(part * 144, 144)
        return pltpu.make_async_remote_copy(
            src_ref=v_ref.at[p, vb, r],
            dst_ref=(up_ref if p == 0 else dn_ref).at[vb, r],
            send_sem=fsend.at[part, p, vb], recv_sem=frecv.at[part, p, vb],
            device_id=(s_prev if p == 0 else s_next, k), device_id_type=MESH)

    line = (xh * 2 + xl) * 4 + z
    lane1 = lane_of((8, 128))
    low1 = lane1 < 64
    for mm in range(2):
        for place in range(3):
            plane = 4 * y + 2 * c + (jnp.where(low1, 0, 1) if place == 2 else place)
            row = 2 * line + (2 if place == 2 else jnp.where(low1, 0, 1))
            col = lane1 & 63
            n = (((mom_ref[mm, 0] * plane) & 15) * 4 + ((mom_ref[mm, 1] * row) & 31) * 2
                 + ((mom_ref[mm, 2] * col) & 63)) & 63
            theta = n.astype(F32) * (2.0 * jnp.pi / 64)
            tab[mm, place, 0] = jnp.cos(theta)
            tab[mm, place, 1] = jnp.sin(theta)

    rows = 16
    lane = lane_of((rows, 128))
    low = lane < 64
    col = lane & 63

    def tools(vb, sub):
        at = pl.multiple_of(vb * 48 + sub * rows, rows)

        def comp(ref, reim, col_, *lead):
            first = pl.multiple_of(reim * 144 + col_ * 48 + sub * rows, rows)
            return ref[(*lead, vb, pl.ds(first, rows), slice(None))]

        def link(ref, mu_, dagger, *lead):
            def get(i, j):
                a, b = (j, i) if dagger else (i, j)
                r = mu_ * 18 + a * 3 + b
                ur = ref[(*lead, pl.ds(r, 1), slice(None))]
                ui = ref[(*lead, pl.ds(r + 9, 1), slice(None))]
                return ur, (-ui if dagger else ui)
            return get

        def put_right(mu_, place, cc, dr, di):
            kk = pl.ds((6 + cc if place == 2 else cc * 2 + place) * 128, 128)
            to = right1 if mu_ == 1 else right02
            off = pl.ds(pl.multiple_of(at + (384 if mu_ == 2 else 0), rows), rows)
            for i, t in enumerate((dr, di - dr, dr + di)):
                hi, lo = halves(t)
                to[i, 0, off, kk] = hi
                to[i, 1, off, kk] = lo

        return at, comp, link, put_right

    def vectors_of(comp):
        return [[(comp(v_ref, 0, cc, p), comp(v_ref, 1, cc, p)) for cc in range(3)] for p in range(2)]

    def put_left(at, place, field):
        for mm in range(2):
            co, si = tab[mm, place, 0, 0:1], tab[mm, place, 1, 0:1]
            for cc in range(3):
                vr, vi = field[cc]
                lr = vr * co - vi * si
                li = -(vr * si + vi * co)
                kk = pl.ds((6 + cc if place == 2 else cc * 2 + place) * 128, 128)
                for i, t in enumerate((lr + li, lr, li)):
                    hi, lo = halves(t)
                    left[mm, i, 0, pl.ds(at, rows), kk] = hi
                    left[mm, i, 1, pl.ds(at, rows), kk] = lo

    def inside(vb, sub):
        at, comp, link, put_right = tools(vb, sub)
        v = vectors_of(comp)

        def ahead(t):
            return jnp.where(col == 63, pltpu.roll(t, 63, 1), pltpu.roll(t, 127, 1))

        def behind(t):
            return jnp.where(col == 0, pltpu.roll(t, 65, 1), pltpu.roll(t, 1, 1))

        for p in range(2):
            put_left(at, p, v[p])
            fwd = apply_link(link(lk_ref, 2, False, p), [(ahead(a), ahead(b)) for a, b in v[p]])
            bwd = apply_link(link(lk_ref, 2, True, p), v[p])
            for cc in range(3):
                put_right(2, p, cc, fwd[cc][0] - behind(bwd[cc][0]),
                          fwd[cc][1] - behind(bwd[cc][1]))

    def along(vb, sub):
        at, comp, link, put_right = tools(vb, sub)
        v = vectors_of(comp)
        packed = []
        for p in range(2):
            packed.append([
                v_ref[p, vb, pl.ds(pl.multiple_of(288 + cc * 48 + sub * rows, rows), rows), :]
                for cc in range(3)])
        put_left(at, 2, [
            (jnp.where(low, packed[0][cc], pltpu.roll(packed[1][cc], 64, 1)),
             jnp.where(low, pltpu.roll(packed[0][cc], 64, 1), packed[1][cc]))
            for cc in range(3)])
        spill = []
        for p in range(2):
            shifted = []
            for cc in range(3):
                vr, vi = v[p][cc]
                shifted.append((
                    pltpu.roll(jnp.where(low, packed[p][cc], vr), 64, 1),
                    jnp.where(low, pltpu.roll(vi, 64, 1), packed[p][cc])))
            fwd = apply_link(link(lk_ref, 1, False, p), shifted)
            bwd = apply_link(link(lk_ref, 1, True, p), v[p])
            turned = []
            for cc in range(3):
                tr, ti = pltpu.roll(bwd[cc][0], 64, 1), pltpu.roll(bwd[cc][1], 64, 1)
                turned.append((tr, ti))
                put_right(1, p, cc, fwd[cc][0] - jnp.where(low, 0.0, tr),
                          fwd[cc][1] - jnp.where(low, 0.0, ti))
            spill.append((bwd, turned))
        for cc in range(3):
            put_right(1, 2, cc,
                      -jnp.where(low, spill[0][1][cc][0], spill[1][0][cc][0]),
                      -jnp.where(low, spill[0][1][cc][1], spill[1][0][cc][1]))

    def across(vb, sub):
        at, comp, link, put_right = tools(vb, sub)
        v = [[(comp(v_ref, 0, cc, p), comp(v_ref, 1, cc, p)) for cc in range(3)] for p in range(2)]
        above = [(comp(up_ref, 0, cc), comp(up_ref, 1, cc)) for cc in range(3)]
        below = [(comp(dn_ref, 0, cc), comp(dn_ref, 1, cc)) for cc in range(3)]
        for p in range(2):
            fwd = apply_link(link(lk_ref, 0, False, p), v[1] if p == 0 else above)
            bwd = (apply_link(link(ulo_ref, 0, True), below) if p == 0
                   else apply_link(link(lk_ref, 0, True, 0), v[0]))
            for cc in range(3):
                put_right(0, p, cc, fwd[cc][0] - bwd[cc][0], fwd[cc][1] - bwd[cc][1])

    def arrivals(other):
        number = 0
        for far in range(2):
            for low_ in range(2):
                digits = [
                    xs_ * 4 + dz for dx, dz in STEPS for xs_ in range(2)
                    if (2 * far + low_ - xs_) % 4 == dx]
                value = sum(t * 8 ** n for n, t in enumerate(digits))
                hit = jnp.logical_and((xh != c) == ((far == 1) != other), xl == low_)
                number = jnp.where(hit, value, number)
        return number

    def vector_block(number):
        digit = number % 8
        return digit // 4 * 4 + (z + 4 - digit % 4) % 4

    def take_real(t, carry):
        number, steps = carry
        steps = put_two(t, 1, steps)
        vb = vector_block(number)
        for p in range(2):
            arrived(p, vb, 0)
            hand(p, vb, 0).start()
        return number // 8, steps

    def take(t, carry):
        number, steps = carry
        steps = put_two(t, 2, steps)
        vb = vector_block(number)
        for p in range(2):
            arrived(p, vb, 1)
            hand(p, vb, 1).start()

        def sub_loop(sub, _):
            inside(vb, sub)
            return 0

        lax.fori_loop(0, 3, sub_loop, 0)
        return number // 8, steps

    begin = arrivals(False), tuple(jnp.int32(n) for n in packed_steps)
    lax.fori_loop(0, 8, take_real, begin)
    lax.fori_loop(0, 8, take, begin)

    def join(t, number):
        vb = vector_block(number)
        for p in range(2):
            hand(p, vb, 0).wait_recv()
            hand(p, vb, 1).wait_recv()

        def sub_loop(sub, _):
            across(vb, sub)
            return 0

        lax.fori_loop(0, 3, sub_loop, 0)
        return number // 8

    def late(t, number):
        vb = vector_block(number)
        for p in range(2):
            arrived(p, vb, 2)

        def sub_loop(sub, _):
            along(vb, sub)
            return 0

        lax.fori_loop(0, 3, sub_loop, 0)
        return number // 8

    dims = (((1,), (1,)), ((), ()))
    dot = functools.partial(lax.dot_general, dimension_numbers=dims, preferred_element_type=F32)

    def one(m, i):
        lh, ll = left[m, i, 0], left[m, i, 1]
        rh, rl = right1[i, 0], right1[i, 1]
        return (dot(lh, rh) + dot(lh, rl) + dot(ll, rh)).reshape(8, 2, 24, 384)

    def one_real(m):
        k1 = one(m, 0)
        e_ref[m, 1] = k1
        e_ref[m, 0] = k1 - one(m, 2)
        core_copy(m, 0).start()

    def one_imag(m):
        e_ref[m, 1] += one(m, 1)
        core_copy(m, 1).start()

    def pair(m, i):
        d = pl.ds(0, 768)
        lh, ll = left[m, i, 0, :, d], left[m, i, 1, :, d]
        rh, rl = right02[i, 0], right02[i, 1]
        t = dot(lh, rh) + dot(lh, rl) + dot(ll, rh)
        return t[:, 0:384].reshape(8, 2, 24, 384), t[:, 384:768].reshape(8, 2, 24, 384)

    def pair_real(m):
        b = 2 + 2 * m
        for n, t in enumerate(pair(m, 0)):
            e_ref[b + n, 1] = t
        for n, t in enumerate(pair(m, 2)):
            e_ref[b + n, 0] = e_ref[b + n, 1] - t
            core_copy(b + n, 0).start()

    def pair_imag(m):
        b = 2 + 2 * m
        for n, t in enumerate(pair(m, 1)):
            e_ref[b + n, 1] += t
            core_copy(b + n, 1).start()

    def core_copy(b, ri):
        return pltpu.make_async_remote_copy(
            src_ref=e_ref.at[b, ri, :, 1 - c], dst_ref=cin.at[b, ri], send_sem=csend.at[b, ri],
            recv_sem=crecv.at[b, ri], device_id=partner, device_id_type=MESH)

    slot = {2: 0, 3: 1, 0: 2, 4: 3, 1: 0, 5: 1}

    def rows_first(b, d, ri):
        at, to = (z, on_z) if b in (2, 3) else (y, on_y)
        return pltpu.make_async_remote_copy(
            src_ref=cs.at[b, ri, (at + d) % 4], dst_ref=yin.at[slot[b], d - 1, ri],
            send_sem=asend.at[b, 3 * ri + d - 1], recv_sem=arecv.at[b, 3 * ri + d - 1],
            device_id=to(d), device_id_type=MESH)

    def x_first(b, d):
        xt = (x + d) % 4
        return pltpu.make_async_remote_copy(
            src_ref=cs.at[b, xt % 2, :, xt // 2], dst_ref=xin.at[slot[b], d - 1],
            send_sem=asend.at[b, d - 1], recv_sem=arecv.at[b, d - 1],
            device_id=on_x(d), device_id_type=MESH)

    def by_rows(b):
        return b not in (1, 5)

    def second(b, d):
        if by_rows(b):
            xt = (x + d) % 4
            src, to = ys.at[slot[b], xt % 2, xt // 2], on_x(d)
        else:
            src, to = xs.at[slot[b], (y + d) % 4], on_y(d)
        return pltpu.make_async_remote_copy(
            src_ref=src, dst_ref=lin.at[b, d - 1], send_sem=bsend.at[b, d - 1],
            recv_sem=brecv.at[b, d - 1], device_id=to, device_id_type=MESH)

    def third(n, kt):
        at = xl * 4 + y if n == 1 else k
        return pltpu.make_async_remote_copy(
            src_ref=zst.at[n, kt], dst_ref=zin.at[n, at], send_sem=zsend.at[n, kt],
            recv_sem=zrecv.at[n, at], device_id=(s_turned if n == 1 else s, kt), device_id_type=MESH)

    def away(n, kt):
        return jnp.logical_or(y != z, kt != k) if n == 1 else kt != k

    def over_core(b, ri):
        core_copy(b, ri).wait_recv()
        for i in range(8):
            cs[b, ri, i // 2, i % 2] = e_ref[b, ri, i, c] + cin[b, ri, i]
        for d in (1, 2, 3):
            if by_rows(b):
                rows_first(b, d, ri).start()
            else:

                @pl.when((x + d) % 2 == ri)
                def _():
                    x_first(b, d).start()

    def over_first(b):
        n = slot[b]
        if by_rows(b):
            q = z if b in (2, 3) else y
            for ri in range(2):
                for d in (1, 2, 3):
                    rows_first(b, d, ri).wait_recv()
                for g in range(2):
                    ys[n, ri, g] = (cs[b, ri, q, g] + yin[n, 0, ri, g]) + (
                        yin[n, 1, ri, g] + yin[n, 2, ri, g])
        else:
            for d in (1, 2, 3):
                x_first(b, d).wait_recv()
            for i in range(4):
                xs[n, i] = (cs[b, xl, i, xh] + xin[n, 0, i]) + (xin[n, 1, i] + xin[n, 2, i])
        for d in (1, 2, 3):
            second(b, d).start()

    def over_second(n):
        sums = []
        for b in (2 * n, 2 * n + 1):
            for d in (1, 2, 3):
                second(b, d).wait_recv()
            own = ys[slot[b], xl, xh] if by_rows(b) else xs[slot[b], y]
            sums.append((own + lin[b, 0]) + (lin[b, 1] + lin[b, 2]))
        first_half = lane_of((24, 128)) < 64
        for kt in range(8):
            zst[n, kt] = jnp.where(
                first_half,
                pltpu.roll(sums[0], (384 - 48 * kt) % 384, 1)[:, 0:128],
                pltpu.roll(sums[1], (448 - 48 * kt) % 384, 1)[:, 0:128])

            @pl.when(away(n, kt))
            def _():
                third(n, kt).start()

        if n == 1:

            @pl.when(y == z)
            def _():
                zin[n, k] = zst[n, k]
        else:
            zin[n, k] = zst[n, k]

    ulo.wait_recv()
    lax.fori_loop(0, 8, join, arrivals(True))
    pair_real(0)
    pair_imag(0)
    over_core(2, 0)
    over_core(3, 0)
    pair_real(1)
    over_core(2, 1)
    over_core(3, 1)
    pair_imag(1)
    over_core(4, 0)
    over_core(5, 0)
    lax.fori_loop(0, 8, late, arrivals(False))
    over_core(4, 1)
    over_core(5, 1)
    one_real(0)
    one_imag(0)
    over_core(0, 0)
    over_first(2)
    over_first(3)
    one_real(1)
    over_core(0, 1)
    over_first(4)
    over_first(5)
    one_imag(1)
    over_core(1, 0)
    over_core(1, 1)
    over_second(1)
    over_first(0)
    over_second(2)
    over_first(1)
    over_second(0)

    def arrive(n):
        for kt in range(8):

            @pl.when(away(n, kt))
            def _():
                pltpu.make_async_copy(zin.at[n, kt], zin.at[n, kt], zrecv.at[n, kt]).wait()

    for n in range(3):
        arrive(n)
    done = {}
    for n in range(3):
        for ri in range(2):
            t = (zin[n, 4 * ri] + zin[n, 4 * ri + 1]) + (zin[n, 4 * ri + 2] + zin[n, 4 * ri + 3])
            done[2 * n, ri] = t[:, 0:48]
            done[2 * n + 1, ri] = pltpu.roll(t, 64, 1)[:, 0:48]
    for m in range(2):
        for ri in range(2):
            d0, d1, d2 = done[2 + 2 * m, ri], done[m, ri], done[3 + 2 * m, ri]
            for n in range(3):
                d = dir_ref[n]
                out_ref[m, n, ri] = jnp.where(d == 0, d0, jnp.where(d == 1, d1, d2))
    for n in range(3):
        for kt in range(8):

            @pl.when(away(n, kt))
            def _():
                third(n, kt).wait_send()
    for b in range(6):
        for ri in range(2):
            core_copy(b, ri).wait_send()
        for d in (1, 2, 3):
            second(b, d).wait_send()
            if by_rows(b):
                rows_first(b, d, 0).wait_send()
                rows_first(b, d, 1).wait_send()
            else:
                x_first(b, d).wait_send()

    def finish(i, _):
        for p in range(2):
            hand(p, i, 0).wait_send()
            hand(p, i, 1).wait_send()
        return 0

    lax.fori_loop(0, 8, finish, 0)
    ulo.wait_send()
    for xt in range(2):

        @pl.when(jnp.logical_not(jnp.logical_and(selfish, xh == xt)))
        def _():
            link_copy(xt).wait_send()

    def sent(i):
        st, kt, _j = target(i)

        @pl.when(jnp.logical_or(st != s, kt != k))
        def _():
            for part in range(3):
                main_copy(i, part).wait_send()

    for i in range(16):
        sent(i)


def elementals(vectors, links, momenta, directions):
    dma = pltpu.SemaphoreType.DMA
    smem = pl.BlockSpec(memory_space=pltpu.SMEM)
    return pl.pallas_call(
        kernel,
        out_shape=jax.ShapeDtypeStruct((2, 3, 2, 24, 48), F32),
        in_specs=[smem, smem, HBM, VMEM],
        out_specs=VMEM,
        scratch_shapes=[
            pltpu.VMEM((288 * 16, 128), F32),
            dma(()),
            pltpu.VMEM((16, 432, 128), F32),
            pltpu.VMEM((2, 56, 128), F32),
            pltpu.VMEM((2, 8, 432, 128), F32),
            pltpu.VMEM((8, 288, 128), F32),
            pltpu.VMEM((8, 288, 128), F32),
            pltpu.VMEM((2, 56, 128), F32),
            pltpu.VMEM((24, 128), F32),
            pltpu.VMEM((2, 3, 2, 384, 1152), BF16),
            pltpu.VMEM((3, 2, 768, 768), BF16),
            pltpu.VMEM((3, 2, 384, 1152), BF16),
            pltpu.VMEM((2, 3, 2, 8, 128), F32),
            pltpu.VMEM((6, 2, 8, 2, 24, 384), F32),
            pltpu.VMEM((6, 2, 8, 24, 384), F32),
            pltpu.VMEM((6, 2, 4, 2, 24, 384), F32),
            pltpu.VMEM((4, 3, 2, 2, 24, 384), F32),
            pltpu.VMEM((4, 2, 2, 24, 384), F32),
            pltpu.VMEM((2, 3, 4, 24, 384), F32),
            pltpu.VMEM((2, 4, 24, 384), F32),
            pltpu.VMEM((3, 8, 24, 128), F32),
            pltpu.VMEM((3, 8, 24, 128), F32),
            pltpu.VMEM((6, 3, 24, 384), F32),
            dma((3, 16)), dma((3, 16)), dma((2,)), dma((2,)),
            dma((2, 2, 8)), dma((2, 2, 8)), dma(()), dma(()),
            dma((6, 2)), dma((6, 2)), dma((6, 6)), dma((6, 6)), dma((6, 3)), dma((6, 3)),
            dma((3, 8)), dma((3, 8)),
        ],
        compiler_params=pltpu.CompilerParams(
            collective_id=0, has_side_effects=True, vmem_limit_bytes=60 << 20),
        cost_estimate=pl.CostEstimate(flops=2 * 18 * 3 * 384 * 384 * 896, bytes_accessed=6 << 20, transcendentals=0),
        name="elementals",
    )(momenta, directions, vectors.reshape(288 * 16, 128), links.reshape(54 * 16, 128))


def solution(mesh):
    placed = (
        P(None, None, "vec", "space", None),
        P(None, None, None, None, "space", None),
        P(),
        P(),
    )
    return jax.shard_map(
        elementals,
        mesh=mesh,
        in_specs=placed,
        out_specs=P(None, None, None, "space", "vec"),
        check_vma=False,
    )
```

```python
import functools

import jax
import jax.numpy as jnp
from jax import lax
from jax.experimental import pallas as pl
from jax.experimental.pallas import tpu as pltpu
from jax.sharding import PartitionSpec as P

MESH = pl.DeviceIdType.MESH
F32 = jnp.float32
BF16 = jnp.bfloat16
VMEM = pl.BlockSpec(memory_space=pltpu.VMEM)
HBM = pl.BlockSpec(memory_space=pl.ANY)


def coords():
    s, k = lax.axis_index("space"), lax.axis_index("vec")
    return s // 4, (s // 2) % 2, s % 2, k // 4, k % 4


def lane_of(shape):
    return lax.broadcasted_iota(jnp.int32, shape, len(shape) - 1)


STEPS = ((1, 0), (0, 1), (3, 0), (0, 3), (2, 0), (0, 2), (1, 1), (3, 3),
         (1, 3), (3, 1), (1, 2), (2, 1), (3, 2), (2, 3), (2, 2), (0, 0))


def halves(t):
    hi = t.astype(BF16)
    return hi, (t - hi.astype(F32)).astype(BF16)


def apply_link(link, field):
    out = []
    for i in range(3):
        re = im = None
        for j in range(3):
            ur, ui = link(i, j)
            fr, fi = field[j]
            a = ur * fr - ui * fi
            b = ur * fi + ui * fr
            re = a if re is None else re + a
            im = b if im is None else im + b
        out.append((re, im))
    return out


def kernel(mom_ref, dir_ref, x_hbm, u_ref, out_ref,
           x_ref, xsem, stage, lstage, v_ref, up_ref, dn_ref, lk_ref, ulo_ref,
           left, right02, right1, tab, e_ref, cin, cs, yin, ys, xin, xs, zst, zin, lin,
           send, recv, lsend, lrecv, fsend, frecv, usend, urecv,
           csend, crecv, asend, arecv, bsend, brecv, zsend, zrecv):
    y, xh, c, xl, z = coords()
    s, k = lax.axis_index("space"), lax.axis_index("vec")
    x = xh * 2 + xl
    selfish = c == xh

    def dev(y_, x_, c_, z_):
        return (y_ * 2 + x_ // 2) * 2 + c_, (x_ % 2) * 4 + z_

    def on_y(d):
        return dev((y + d) % 4, x, c, z)

    def on_x(d):
        return dev(y, (x + d) % 4, c, z)

    def on_z(d):
        return dev(y, x, c, (z + d) % 4)

    partner = dev(y, x, 1 - c, z)
    s_turned = (z * 2 + xh) * 2 + c
    q = 2 * y + c
    qn, qp = (q + 1) % 8, (q + 7) % 8
    s_next = (qn // 2 * 2 + xh) * 2 + qn % 2
    s_prev = (qp // 2 * 2 + xh) * 2 + qp % 2

    def target(i, step=None):
        dx, dz = STEPS[i] if step is None else step
        xt, zt = (x + dx) % 4, (z + dz) % 4
        return (y * 2 + xt // 2) * 2 + xh, (xt % 2) * 4 + zt, xt * 4 + zt

    def origin(i):
        return (y * 2 + c) * 2 + i % 2, i // 2

    fetch = pltpu.make_async_copy(x_hbm, x_ref, xsem)
    fetch.start()
    barrier = pltpu.get_barrier_semaphore()

    def greet(i):
        st, kt, _j = target(i)

        @pl.when(jnp.logical_or(st != s, kt != k))
        def _():
            pl.semaphore_signal(barrier, inc=1, device_id=(st, kt), device_id_type=MESH)

        so, ko = origin(i)

        @pl.when(jnp.logical_or(so != s, ko != k))
        def _():
            pl.semaphore_signal(barrier, inc=1, device_id=(so, ko), device_id_type=MESH)

    for i in range(16):
        greet(i)
    pl.semaphore_signal(barrier, inc=1, device_id=(s_next, k), device_id_type=MESH)
    pl.semaphore_signal(barrier, inc=1, device_id=(s_prev, k), device_id_type=MESH)

    pl.semaphore_signal(barrier, inc=1, device_id=partner, device_id_type=MESH)
    for d in (1, 2, 3):
        for on in (on_y, on_x):
            pl.semaphore_signal(barrier, inc=1, device_id=on(d), device_id_type=MESH)
    for kt in range(8):

        @pl.when(kt != k)
        def _():
            pl.semaphore_signal(barrier, inc=1, device_id=(s, kt), device_id_type=MESH)

        @pl.when(jnp.logical_or(s_turned != s, kt != k))
        def _():
            pl.semaphore_signal(barrier, inc=1, device_id=(s_turned, kt), device_id_type=MESH)

        so, ko = (kt % 4 * 2 + xh) * 2 + c, kt // 4 * 4 + y

        @pl.when(jnp.logical_or(so != s, ko != k))
        def _():
            pl.semaphore_signal(barrier, inc=1, device_id=(so, ko), device_id_type=MESH)

    for xt in range(2):
        j = (xt * 2 + xl) * 4 + z
        lstage[xt, 48:56, :] = jnp.zeros((8, 128), F32)
        lstage[xt, 0:54, :] = u_ref[pl.ds(j, 54, stride=16), :]
    pl.semaphore_wait(barrier, jnp.where(selfish, 62, 64) - jnp.where(y == z, 2, 0))

    def link_copy(xt):
        return pltpu.make_async_remote_copy(
            src_ref=lstage.at[xt], dst_ref=lk_ref.at[c], send_sem=lsend.at[xt],
            recv_sem=lrecv.at[c], device_id=((y * 2 + xt) * 2 + xh, k), device_id_type=MESH)

    for xt in range(2):
        mine = jnp.logical_and(selfish, xh == xt)

        @pl.when(mine)
        def _():
            pltpu.make_async_copy(lstage.at[xt], lk_ref.at[c], lrecv.at[c]).start()

        @pl.when(jnp.logical_not(mine))
        def _():
            link_copy(xt).start()


    def main_copy(i, part, step=None):
        st, kt, j = target(i, step)
        r = pl.ds(part * 144, 144)
        return pltpu.make_async_remote_copy(
            src_ref=stage.at[i, r], dst_ref=v_ref.at[c, k, r], send_sem=send.at[part, i],
            recv_sem=recv.at[part, c * 8 + k], device_id=(st, kt), device_id_type=MESH)

    def arrived(p, vb, part):
        r = pl.ds(part * 144, 144)
        pltpu.make_async_copy(
            v_ref.at[p, vb, r], v_ref.at[p, vb, r], recv.at[part, p * 8 + vb]).wait()

    def put(i, part, step=None):
        st, kt, j = target(i, step)
        r = pl.ds(part * 144, 144)
        if part < 2:
            stage[i, r, :] = x_ref[pl.ds(part * 144 * 16 + j, 144, stride=16), :]
        else:
            nxt = (j + 1) % 16
            re = x_ref[pl.ds(nxt, 144, stride=16), :]
            im = x_ref[pl.ds(144 * 16 + nxt, 144, stride=16), :]
            stage[i, r, :] = jnp.where(lane_of((144, 128)) < 64, re, pltpu.roll(im, 64, 1))
        mine = jnp.logical_and(st == s, kt == k)

        @pl.when(mine)
        def _():
            pltpu.make_async_copy(
                stage.at[i, r], v_ref.at[c, k, r], recv.at[part, c * 8 + k]).start()

        @pl.when(jnp.logical_not(mine))
        def _():
            main_copy(i, part, step).start()

    fetch.wait()
    for i in range(16):
        put(i, 0)

    packed_steps = tuple(
        sum(STEPS[2 * n + odd][axis] * 4 ** n for n in range(8))
        for odd in range(2) for axis in range(2))

    def put_two(t, part, steps):
        for odd in range(2):
            put(2 * t + odd, part, (steps[2 * odd] % 4, steps[2 * odd + 1] % 4))
        return tuple(n // 4 for n in steps)

    for p in range(2):
        pltpu.make_async_copy(lk_ref.at[p], lk_ref.at[p], lrecv.at[p]).wait()
    ulo = pltpu.make_async_remote_copy(
        src_ref=lk_ref.at[1, pl.ds(0, 24)], dst_ref=ulo_ref, send_sem=usend,
        recv_sem=urecv, device_id=(s_next, k), device_id_type=MESH)
    ulo.start()

    def hand(p, vb, part):
        r = pl.ds(part * 144, 144)
        return pltpu.make_async_remote_copy(
            src_ref=v_ref.at[p, vb, r],
            dst_ref=(up_ref if p == 0 else dn_ref).at[vb, r],
            send_sem=fsend.at[part, p, vb], recv_sem=frecv.at[part, p, vb],
            device_id=(s_prev if p == 0 else s_next, k), device_id_type=MESH)

    line = (xh * 2 + xl) * 4 + z
    lane1 = lane_of((8, 128))
    low1 = lane1 < 64
    for mm in range(2):
        for place in range(3):
            plane = 4 * y + 2 * c + (jnp.where(low1, 0, 1) if place == 2 else place)
            row = 2 * line + (2 if place == 2 else jnp.where(low1, 0, 1))
            col = lane1 & 63
            n = (((mom_ref[mm, 0] * plane) & 15) * 4 + ((mom_ref[mm, 1] * row) & 31) * 2
                 + ((mom_ref[mm, 2] * col) & 63)) & 63
            theta = n.astype(F32) * (2.0 * jnp.pi / 64)
            tab[mm, place, 0] = jnp.cos(theta)
            tab[mm, place, 1] = jnp.sin(theta)

    rows = 16
    lane = lane_of((rows, 128))
    low = lane < 64
    col = lane & 63

    def tools(vb, sub):
        at = pl.multiple_of(vb * 48 + sub * rows, rows)

        def comp(ref, reim, col_, *lead):
            first = pl.multiple_of(reim * 144 + col_ * 48 + sub * rows, rows)
            return ref[(*lead, vb, pl.ds(first, rows), slice(None))]

        def link(ref, mu_, dagger, *lead):
            def get(i, j):
                a, b = (j, i) if dagger else (i, j)
                r = mu_ * 18 + a * 3 + b
                ur = ref[(*lead, pl.ds(r, 1), slice(None))]
                ui = ref[(*lead, pl.ds(r + 9, 1), slice(None))]
                return ur, (-ui if dagger else ui)
            return get

        def put_right(mu_, place, cc, dr, di):
            kk = pl.ds((6 + cc if place == 2 else cc * 2 + place) * 128, 128)
            to = right1 if mu_ == 1 else right02
            off = pl.ds(pl.multiple_of(at + (384 if mu_ == 2 else 0), rows), rows)
            for i, t in enumerate((dr, di - dr, dr + di)):
                hi, lo = halves(t)
                to[i, 0, off, kk] = hi
                to[i, 1, off, kk] = lo

        return at, comp, link, put_right

    def vectors_of(comp):
        return [[(comp(v_ref, 0, cc, p), comp(v_ref, 1, cc, p)) for cc in range(3)] for p in range(2)]

    def put_left(at, place, field):
        for mm in range(2):
            co, si = tab[mm, place, 0, 0:1], tab[mm, place, 1, 0:1]
            for cc in range(3):
                vr, vi = field[cc]
                lr = vr * co - vi * si
                li = -(vr * si + vi * co)
                kk = pl.ds((6 + cc if place == 2 else cc * 2 + place) * 128, 128)
                for i, t in enumerate((lr + li, lr, li)):
                    hi, lo = halves(t)
                    left[mm, i, 0, pl.ds(at, rows), kk] = hi
                    left[mm, i, 1, pl.ds(at, rows), kk] = lo

    def inside(vb, sub):
        at, comp, link, put_right = tools(vb, sub)
        v = vectors_of(comp)

        def ahead(t):
            return jnp.where(col == 63, pltpu.roll(t, 63, 1), pltpu.roll(t, 127, 1))

        def behind(t):
            return jnp.where(col == 0, pltpu.roll(t, 65, 1), pltpu.roll(t, 1, 1))

        for p in range(2):
            put_left(at, p, v[p])
            fwd = apply_link(link(lk_ref, 2, False, p), [(ahead(a), ahead(b)) for a, b in v[p]])
            bwd = apply_link(link(lk_ref, 2, True, p), v[p])
            for cc in range(3):
                put_right(2, p, cc, fwd[cc][0] - behind(bwd[cc][0]),
                          fwd[cc][1] - behind(bwd[cc][1]))

    def along(vb, sub):
        at, comp, link, put_right = tools(vb, sub)
        v = vectors_of(comp)
        packed = []
        for p in range(2):
            packed.append([
                v_ref[p, vb, pl.ds(pl.multiple_of(288 + cc * 48 + sub * rows, rows), rows), :]
                for cc in range(3)])
        put_left(at, 2, [
            (jnp.where(low, packed[0][cc], pltpu.roll(packed[1][cc], 64, 1)),
             jnp.where(low, pltpu.roll(packed[0][cc], 64, 1), packed[1][cc]))
            for cc in range(3)])
        spill = []
        for p in range(2):
            shifted = []
            for cc in range(3):
                vr, vi = v[p][cc]
                shifted.append((
                    pltpu.roll(jnp.where(low, packed[p][cc], vr), 64, 1),
                    jnp.where(low, pltpu.roll(vi, 64, 1), packed[p][cc])))
            fwd = apply_link(link(lk_ref, 1, False, p), shifted)
            bwd = apply_link(link(lk_ref, 1, True, p), v[p])
            turned = []
            for cc in range(3):
                tr, ti = pltpu.roll(bwd[cc][0], 64, 1), pltpu.roll(bwd[cc][1], 64, 1)
                turned.append((tr, ti))
                put_right(1, p, cc, fwd[cc][0] - jnp.where(low, 0.0, tr),
                          fwd[cc][1] - jnp.where(low, 0.0, ti))
            spill.append((bwd, turned))
        for cc in range(3):
            put_right(1, 2, cc,
                      -jnp.where(low, spill[0][1][cc][0], spill[1][0][cc][0]),
                      -jnp.where(low, spill[0][1][cc][1], spill[1][0][cc][1]))

    def across(vb, sub):
        at, comp, link, put_right = tools(vb, sub)
        v = [[(comp(v_ref, 0, cc, p), comp(v_ref, 1, cc, p)) for cc in range(3)] for p in range(2)]
        above = [(comp(up_ref, 0, cc), comp(up_ref, 1, cc)) for cc in range(3)]
        below = [(comp(dn_ref, 0, cc), comp(dn_ref, 1, cc)) for cc in range(3)]
        for p in range(2):
            fwd = apply_link(link(lk_ref, 0, False, p), v[1] if p == 0 else above)
            bwd = (apply_link(link(ulo_ref, 0, True), below) if p == 0
                   else apply_link(link(lk_ref, 0, True, 0), v[0]))
            for cc in range(3):
                put_right(0, p, cc, fwd[cc][0] - bwd[cc][0], fwd[cc][1] - bwd[cc][1])

    def arrivals(other):
        number = 0
        for far in range(2):
            for low_ in range(2):
                digits = [
                    xs_ * 4 + dz for dx, dz in STEPS for xs_ in range(2)
                    if (2 * far + low_ - xs_) % 4 == dx]
                value = sum(t * 8 ** n for n, t in enumerate(digits))
                hit = jnp.logical_and((xh != c) == ((far == 1) != other), xl == low_)
                number = jnp.where(hit, value, number)
        return number

    def vector_block(number):
        digit = number % 8
        return digit // 4 * 4 + (z + 4 - digit % 4) % 4

    def take_real(t, carry):
        number, steps = carry
        steps = put_two(t, 1, steps)
        vb = vector_block(number)
        for p in range(2):
            arrived(p, vb, 0)
            hand(p, vb, 0).start()
        return number // 8, steps

    def take(t, carry):
        number, steps = carry
        vb = vector_block(number)
        for p in range(2):
            arrived(p, vb, 1)
            hand(p, vb, 1).start()
        steps = put_two(t, 2, steps)

        def sub_loop(sub, _):
            inside(vb, sub)
            return 0

        lax.fori_loop(0, 3, sub_loop, 0)
        return number // 8, steps

    begin = arrivals(False), tuple(jnp.int32(n) for n in packed_steps)
    lax.fori_loop(0, 8, take_real, begin)
    lax.fori_loop(0, 8, take, begin)

    def join(t, number):
        vb = vector_block(number)
        for p in range(2):
            hand(p, vb, 0).wait_recv()
            hand(p, vb, 1).wait_recv()

        def sub_loop(sub, _):
            across(vb, sub)
            return 0

        lax.fori_loop(0, 3, sub_loop, 0)
        return number // 8

    def late(t, number):
        vb = vector_block(number)
        for p in range(2):
            arrived(p, vb, 2)

        def sub_loop(sub, _):
            along(vb, sub)
            return 0

        lax.fori_loop(0, 3, sub_loop, 0)
        return number // 8

    dims = (((1,), (1,)), ((), ()))
    dot = functools.partial(lax.dot_general, dimension_numbers=dims, preferred_element_type=F32)

    def one(m, i):
        lh, ll = left[m, i, 0], left[m, i, 1]
        rh, rl = right1[i, 0], right1[i, 1]
        return (dot(lh, rh) + dot(lh, rl) + dot(ll, rh)).reshape(8, 2, 24, 384)

    def one_real(m):
        k1 = one(m, 0)
        e_ref[m, 1] = k1
        e_ref[m, 0] = k1 - one(m, 2)
        core_copy(m, 0).start()

    def one_imag(m):
        e_ref[m, 1] += one(m, 1)
        core_copy(m, 1).start()

    def pair(m, i):
        d = pl.ds(0, 768)
        lh, ll = left[m, i, 0, :, d], left[m, i, 1, :, d]
        rh, rl = right02[i, 0], right02[i, 1]
        t = dot(lh, rh) + dot(lh, rl) + dot(ll, rh)
        return t[:, 0:384].reshape(8, 2, 24, 384), t[:, 384:768].reshape(8, 2, 24, 384)

    def pair_real(m):
        b = 2 + 2 * m
        for n, t in enumerate(pair(m, 0)):
            e_ref[b + n, 1] = t
        for n, t in enumerate(pair(m, 2)):
            e_ref[b + n, 0] = e_ref[b + n, 1] - t
            core_copy(b + n, 0).start()

    def pair_imag(m):
        b = 2 + 2 * m
        for n, t in enumerate(pair(m, 1)):
            e_ref[b + n, 1] += t
            core_copy(b + n, 1).start()

    def core_copy(b, ri):
        return pltpu.make_async_remote_copy(
            src_ref=e_ref.at[b, ri, :, 1 - c], dst_ref=cin.at[b, ri], send_sem=csend.at[b, ri],
            recv_sem=crecv.at[b, ri], device_id=partner, device_id_type=MESH)

    slot = {2: 0, 3: 1, 0: 2, 4: 3, 1: 0, 5: 1}

    def rows_first(b, d, ri):
        at, to = (z, on_z) if b in (2, 3) else (y, on_y)
        return pltpu.make_async_remote_copy(
            src_ref=cs.at[b, ri, (at + d) % 4], dst_ref=yin.at[slot[b], d - 1, ri],
            send_sem=asend.at[b, 3 * ri + d - 1], recv_sem=arecv.at[b, 3 * ri + d - 1],
            device_id=to(d), device_id_type=MESH)

    def x_first(b, d):
        xt = (x + d) % 4
        return pltpu.make_async_remote_copy(
            src_ref=cs.at[b, xt % 2, :, xt // 2], dst_ref=xin.at[slot[b], d - 1],
            send_sem=asend.at[b, d - 1], recv_sem=arecv.at[b, d - 1],
            device_id=on_x(d), device_id_type=MESH)

    def by_rows(b):
        return b not in (1, 5)

    def second(b, d):
        if by_rows(b):
            xt = (x + d) % 4
            src, to = ys.at[slot[b], xt % 2, xt // 2], on_x(d)
        else:
            src, to = xs.at[slot[b], (y + d) % 4], on_y(d)
        return pltpu.make_async_remote_copy(
            src_ref=src, dst_ref=lin.at[b, d - 1], send_sem=bsend.at[b, d - 1],
            recv_sem=brecv.at[b, d - 1], device_id=to, device_id_type=MESH)

    def third(n, kt):
        at = xl * 4 + y if n == 1 else k
        return pltpu.make_async_remote_copy(
            src_ref=zst.at[n, kt], dst_ref=zin.at[n, at], send_sem=zsend.at[n, kt],
            recv_sem=zrecv.at[n, at], device_id=(s_turned if n == 1 else s, kt), device_id_type=MESH)

    def away(n, kt):
        return jnp.logical_or(y != z, kt != k) if n == 1 else kt != k

    def over_core(b, ri):
        core_copy(b, ri).wait_recv()
        for i in range(8):
            cs[b, ri, i // 2, i % 2] = e_ref[b, ri, i, c] + cin[b, ri, i]
        for d in (1, 2, 3):
            if by_rows(b):
                rows_first(b, d, ri).start()
            else:

                @pl.when((x + d) % 2 == ri)
                def _():
                    x_first(b, d).start()

    def over_first(b):
        n = slot[b]
        if by_rows(b):
            q = z if b in (2, 3) else y
            for ri in range(2):
                for d in (1, 2, 3):
                    rows_first(b, d, ri).wait_recv()
                for g in range(2):
                    ys[n, ri, g] = (cs[b, ri, q, g] + yin[n, 0, ri, g]) + (
                        yin[n, 1, ri, g] + yin[n, 2, ri, g])
        else:
            for d in (1, 2, 3):
                x_first(b, d).wait_recv()
            for i in range(4):
                xs[n, i] = (cs[b, xl, i, xh] + xin[n, 0, i]) + (xin[n, 1, i] + xin[n, 2, i])
        for d in (1, 2, 3):
            second(b, d).start()

    def over_second(n):
        sums = []
        for b in (2 * n, 2 * n + 1):
            for d in (1, 2, 3):
                second(b, d).wait_recv()
            own = ys[slot[b], xl, xh] if by_rows(b) else xs[slot[b], y]
            sums.append((own + lin[b, 0]) + (lin[b, 1] + lin[b, 2]))
        first_half = lane_of((24, 128)) < 64
        for kt in range(8):
            zst[n, kt] = jnp.where(
                first_half,
                pltpu.roll(sums[0], (384 - 48 * kt) % 384, 1)[:, 0:128],
                pltpu.roll(sums[1], (448 - 48 * kt) % 384, 1)[:, 0:128])

            @pl.when(away(n, kt))
            def _():
                third(n, kt).start()

        if n == 1:

            @pl.when(y == z)
            def _():
                zin[n, k] = zst[n, k]
        else:
            zin[n, k] = zst[n, k]

    ulo.wait_recv()
    lax.fori_loop(0, 8, join, arrivals(True))
    pair_real(0)
    pair_imag(0)
    over_core(2, 0)
    over_core(3, 0)
    pair_real(1)
    over_core(2, 1)
    over_core(3, 1)
    pair_imag(1)
    over_core(4, 0)
    over_core(5, 0)
    lax.fori_loop(0, 8, late, arrivals(False))
    over_core(4, 1)
    over_core(5, 1)
    one_real(0)
    one_imag(0)
    over_core(0, 0)
    over_first(2)
    over_first(3)
    one_real(1)
    over_core(0, 1)
    over_first(4)
    over_first(5)
    one_imag(1)
    over_core(1, 0)
    over_first(0)
    over_core(1, 1)
    over_second(1)
    over_second(2)
    over_first(1)
    over_second(0)

    def arrive(n):
        for kt in range(8):

            @pl.when(away(n, kt))
            def _():
                pltpu.make_async_copy(zin.at[n, kt], zin.at[n, kt], zrecv.at[n, kt]).wait()

    for n in range(3):
        arrive(n)
    done = {}
    for n in range(3):
        for ri in range(2):
            t = (zin[n, 4 * ri] + zin[n, 4 * ri + 1]) + (zin[n, 4 * ri + 2] + zin[n, 4 * ri + 3])
            done[2 * n, ri] = t[:, 0:48]
            done[2 * n + 1, ri] = pltpu.roll(t, 64, 1)[:, 0:48]
    for m in range(2):
        for ri in range(2):
            d0, d1, d2 = done[2 + 2 * m, ri], done[m, ri], done[3 + 2 * m, ri]
            for n in range(3):
                d = dir_ref[n]
                out_ref[m, n, ri] = jnp.where(d == 0, d0, jnp.where(d == 1, d1, d2))
    for n in range(3):
        for kt in range(8):

            @pl.when(away(n, kt))
            def _():
                third(n, kt).wait_send()
    for b in range(6):
        for ri in range(2):
            core_copy(b, ri).wait_send()
        for d in (1, 2, 3):
            second(b, d).wait_send()
            if by_rows(b):
                rows_first(b, d, 0).wait_send()
                rows_first(b, d, 1).wait_send()
            else:
                x_first(b, d).wait_send()

    def finish(i, _):
        for p in range(2):
            hand(p, i, 0).wait_send()
            hand(p, i, 1).wait_send()
        return 0

    lax.fori_loop(0, 8, finish, 0)
    ulo.wait_send()
    for xt in range(2):

        @pl.when(jnp.logical_not(jnp.logical_and(selfish, xh == xt)))
        def _():
            link_copy(xt).wait_send()

    def sent(i):
        st, kt, _j = target(i)

        @pl.when(jnp.logical_or(st != s, kt != k))
        def _():
            for part in range(3):
                main_copy(i, part).wait_send()

    for i in range(16):
        sent(i)


def elementals(vectors, links, momenta, directions):
    dma = pltpu.SemaphoreType.DMA
    smem = pl.BlockSpec(memory_space=pltpu.SMEM)
    return pl.pallas_call(
        kernel,
        out_shape=jax.ShapeDtypeStruct((2, 3, 2, 24, 48), F32),
        in_specs=[smem, smem, HBM, VMEM],
        out_specs=VMEM,
        scratch_shapes=[
            pltpu.VMEM((288 * 16, 128), F32),
            dma(()),
            pltpu.VMEM((16, 432, 128), F32),
            pltpu.VMEM((2, 56, 128), F32),
            pltpu.VMEM((2, 8, 432, 128), F32),
            pltpu.VMEM((8, 288, 128), F32),
            pltpu.VMEM((8, 288, 128), F32),
            pltpu.VMEM((2, 56, 128), F32),
            pltpu.VMEM((24, 128), F32),
            pltpu.VMEM((2, 3, 2, 384, 1152), BF16),
            pltpu.VMEM((3, 2, 768, 768), BF16),
            pltpu.VMEM((3, 2, 384, 1152), BF16),
            pltpu.VMEM((2, 3, 2, 8, 128), F32),
            pltpu.VMEM((6, 2, 8, 2, 24, 384), F32),
            pltpu.VMEM((6, 2, 8, 24, 384), F32),
            pltpu.VMEM((6, 2, 4, 2, 24, 384), F32),
            pltpu.VMEM((4, 3, 2, 2, 24, 384), F32),
            pltpu.VMEM((4, 2, 2, 24, 384), F32),
            pltpu.VMEM((2, 3, 4, 24, 384), F32),
            pltpu.VMEM((2, 4, 24, 384), F32),
            pltpu.VMEM((3, 8, 24, 128), F32),
            pltpu.VMEM((3, 8, 24, 128), F32),
            pltpu.VMEM((6, 3, 24, 384), F32),
            dma((3, 16)), dma((3, 16)), dma((2,)), dma((2,)),
            dma((2, 2, 8)), dma((2, 2, 8)), dma(()), dma(()),
            dma((6, 2)), dma((6, 2)), dma((6, 6)), dma((6, 6)), dma((6, 3)), dma((6, 3)),
            dma((3, 8)), dma((3, 8)),
        ],
        compiler_params=pltpu.CompilerParams(
            collective_id=0, has_side_effects=True, vmem_limit_bytes=60 << 20),
        cost_estimate=pl.CostEstimate(flops=2 * 18 * 3 * 384 * 384 * 896, bytes_accessed=6 << 20, transcendentals=0),
        name="elementals",
    )(momenta, directions, vectors.reshape(288 * 16, 128), links.reshape(54 * 16, 128))


def solution(mesh):
    placed = (
        P(None, None, "vec", "space", None),
        P(None, None, None, None, "space", None),
        P(),
        P(),
    )
    return jax.shard_map(
        elementals,
        mesh=mesh,
        in_specs=placed,
        out_specs=P(None, None, None, "space", "vec"),
        check_vma=False,
    )
```
